32 devices in a mesh: expert: 4 (over z), dp: 8 (over y, x, core).
Axes of the slice: x: 2, y: 2, z: 4, core: 2. Of those that a mesh axis runs over, the one named last changes fastest.
Arguments:
- tokens: bfloat16 [2048, 4096], P(('expert', 'dp')), may hold values from -6 to 6
- out_grad: bfloat16 [2048, 4096], P(('expert', 'dp')), may hold values from -6 to 6
- routes: int32 [2048, 8], P(('expert', 'dp')), may hold values from 0 to 31, all different within a row; in each aligned block of 64 rows (0 to 63, 64 to 127, ...) at most 24 rows name the same one
- gate_probs: bfloat16 [2048, 8], P(('expert', 'dp')), may hold values from 0.019897461 to 0.5
- doc_ids: int32 [2048], P(('expert', 'dp')), may hold values from 0 to 31, never falling along the last dimension, each value on 1 to 256 neighbouring positions
- w_gate: bfloat16 [32, 4096, 1024], P(('expert', 'dp')), may hold values from -0.09375 to 0.09375
- w_up: bfloat16 [32, 4096, 1024], P(('expert', 'dp')), may hold values from -0.09375 to 0.09375
- proj_hidden: bfloat16 [1024, 32], replicated, may hold values from -0.1875 to 0.1875
- proj_out: bfloat16 [4096, 32], replicated, may hold values from -0.09375 to 0.09375
Outputs:
- sketches: float32 [32, 32, 1024], P(('expert', 'dp'))
The draws below stay inside these ranges and needn't reach their ends.
Inputs may be any that keep to these rules, and one draw needn't show every extreme that they name: `routes`: each row names 8 different experts; among the rows of one device no expert is named by more than 24 rows, and in every draw some device's rows name some expert exactly 24 times. `doc_ids`: never falling along the tokens; every document has 1 to 256 tokens, one exactly 256.
All inputs are finite; a program needn't handle non-finite values.
Results may differ from the reference program's by a relative error of at most 0.005.
Values may be sent and summed in bfloat16 or wider, within the bound.
No kernel may reach another device: no remote copies, remote signals or barrier semaphores. Data moves between devices by JAX's collectives and lax.ppermute only.
A program may use at most 128 MiB of HBM per device.

```python
import math
import jax
import jax.numpy as jnp
import numpy as np
from jax import lax

D = 4096
H = 1024
TOP = 8
R = 32
TOK_DEV = 64
EXPERTS = 32
TOKENS = 2048
CAP = 24
NDOC = 32
DOC_MOST = 256


def levels(own_key, shape, pieces, smallest, high):
    factor_of = 1.0
    for axis_at, blocks in pieces:
        draws = jax.random.uniform(jax.random.fold_in(jax.random.fold_in(own_key, 6), axis_at), (blocks,), jnp.float32, smallest / len(pieces), high / len(pieces))
        factor_of = factor_of * jnp.repeat(jnp.exp(draws), shape[axis_at] // blocks).reshape((-1,) + (1,) * (len(shape) - 1 - axis_at))
    return factor_of


def profile(count, total, bound, lean):
    loads = [(1 << 20) // math.isqrt(rank ** lean) + 1 for rank in range(2, count + 1)]
    surplus, holding = total - bound - (count - 1), [1] * (count - 1)
    while surplus > 0:
        movable = [i for i in range(count - 1) if holding[i] < bound]
        whole, budget = sum([loads[i] for i in movable]), surplus
        for i in movable:
            addition = min(bound - holding[i], max(1, budget * loads[i] // whole), surplus)
            holding[i] = holding[i] + addition
            surplus = surplus - addition
    return np.array([bound] + holding)


def ragged_sizes(stream_key, number_of, total, bound, slope):
    if number_of == 2:
        one = jax.random.randint(stream_key, (), max(1, total - bound), min(bound, total - 1) + 1)
        return jnp.stack([one, total - one])
    sizes = jnp.asarray(profile(number_of, total, bound, slope), jnp.int32)
    pairs = (number_of - 1) // 2
    donor, taker = sizes[1:1 + 2 * pairs:2], sizes[2:2 + 2 * pairs:2]
    room = jnp.minimum(donor - 1, bound - taker)
    passed = jax.random.randint(jax.random.fold_in(stream_key, 1), (pairs,), 0, 1 << 20) % (room + 1)
    sizes = sizes.at[1:1 + 2 * pairs:2].set(donor - passed).at[2:2 + 2 * pairs:2].set(taker + passed)
    return sizes[jax.random.permutation(jax.random.fold_in(stream_key, 2), number_of)]


def shared_out(key, own, number, rows, number_of, top, reach, lean):
    ranking = jax.random.permutation(key, number_of)
    crowded, common = portions_of(number_of, rows * top, reach, lean, True), portions_of(number_of, rows * top, reach, lean, False)
    places = jnp.arange(number_of)

    def named(sizes, rotation):
        used = int((sizes > 0).sum())
        fixed = max(1, used // 4)
        moved = fixed + (places - fixed + rotation * (used - fixed)) % max(1, number_of - fixed)
        return jnp.zeros((number_of,), jnp.int32).at[ranking[jnp.where(places < fixed, places, moved)]].set(jnp.asarray(sizes, jnp.int32))

    sizes = jnp.where(number % 4 == 0, named(crowded, number // 4), named(common, number - number // 4 - 1))
    mixed = jax.random.permutation(jax.random.fold_in(own, 3), number_of)
    giver, sink = mixed[0:number_of // 2 * 2:2], mixed[1:number_of // 2 * 2:2]
    slack = jnp.minimum(sizes[giver] - 1, reach - sizes[sink]) // 2
    slack = jnp.where((giver == ranking[0]) | (sink == ranking[0]) | (sizes[sink] == 0), 0, jnp.maximum(slack, 0))
    moved = jax.random.randint(jax.random.fold_in(own, 4), (number_of // 2,), 0, 1 << 20) % (slack + 1)
    sizes = sizes.at[giver].add(-moved).at[sink].add(moved)
    items = jnp.searchsorted(jnp.cumsum(sizes), jnp.arange(rows * top), side="right").astype(jnp.int32)
    grid = items.reshape(top, rows).T
    grid = grid[jax.random.permutation(jax.random.fold_in(own, 1), rows)]
    rotation = jax.random.randint(jax.random.fold_in(own, 2), (rows, 1), 0, top)
    return jnp.take_along_axis(grid, (jnp.arange(top)[None, :] + rotation) % top, axis=1)


def portions_of(number_of, total, bound, lean, full):
    portions = [(1 << 20) // math.isqrt(rank ** lean) + 1 for rank in range(1, number_of + 1)]
    largest = bound if full else min(bound, max(-(-total // number_of), total * portions[0] // sum(portions)))
    least = 1 if total - largest >= number_of - 1 else 0
    given, rest = [largest] + [least] * (number_of - 1), total - largest - least * (number_of - 1)
    while rest > 0:
        candidates = [i for i in range(1, number_of) if given[i] < largest] or [i for i in range(1, number_of) if given[i] < bound]
        mass, remaining = sum([portions[i] for i in candidates]), rest
        for i in candidates:
            more = min(bound - given[i], max(1, remaining * portions[i] // mass), rest)
            given[i] = given[i] + more
            rest = rest - more
    return np.array(given)


def centred(own_key, extent, scale, most, split=(), kind=jnp.bfloat16):
    entries = jax.random.normal(own_key, extent, jnp.float32) * scale
    if len(split) > 0:
        entries = levels(own_key, extent, split, -0.22, 0.18) * entries
    return jnp.clip(entries, min=-most, max=most).astype(kind)


def setup_inputs(seed: int = 0) -> dict:
    key_list = jax.random.split(jax.random.key(seed), 10)
    tokens = centred(key_list[0], (TOKENS, D), 1.0, 6.0, ((0, 32),))
    out_grad = centred(key_list[1], (TOKENS, D), 1.0, 6.0, ((0, 32),))
    routes_keys = jax.random.split(jax.random.fold_in(key_list[2], 1), TOKENS // TOK_DEV)
    routes_turns = jax.random.permutation(jax.random.fold_in(key_list[2], 3), TOKENS // TOK_DEV)
    routes = jax.vmap(lambda own, number: shared_out(jax.random.fold_in(key_list[2], 2), own, number, TOK_DEV, EXPERTS, TOP, CAP, 2))(routes_keys, routes_turns).reshape((TOKENS, TOP))
    gate_probs = jnp.clip(jnp.exp(math.log(0.5) - 3.224016 * jax.random.uniform(key_list[3], (TOKENS, TOP), jnp.float32) ** levels(key_list[3], (TOKENS, TOP), ((0, 32),), -0.2, 0.2)), 0.019897461, 0.5).astype(jnp.bfloat16)
    doc_ids = jnp.searchsorted(jnp.cumsum(ragged_sizes(key_list[4], NDOC, TOKENS, DOC_MOST, 1)), jnp.arange(TOKENS), side="right").astype(jnp.int32)
    w_gate = centred(key_list[5], (EXPERTS, D, H), D ** -0.5, 0.09375, ((0, 32),))
    w_up = centred(key_list[6], (EXPERTS, D, H), D ** -0.5, 0.09375, ((0, 32),))
    proj_hidden = centred(key_list[7], (H, R), H ** -0.5, 0.1875)
    proj_out = centred(key_list[8], (D, R), D ** -0.5, 0.09375)
    return dict(tokens=tokens, out_grad=out_grad, routes=routes, gate_probs=gate_probs, doc_ids=doc_ids, w_gate=w_gate, w_up=w_up, proj_hidden=proj_hidden, proj_out=proj_out)


pad_unit = 128


def reference(tokens, out_grad, routes, gate_probs, doc_ids, w_gate, w_up, proj_hidden, proj_out):
    pair_count = TOKENS * TOP
    flat_expert = routes.reshape(-1).astype(jnp.int32)
    counts = jnp.zeros((EXPERTS,), jnp.int32).at[flat_expert].add(1)
    padded = (counts + pad_unit - 1) // pad_unit * pad_unit
    padded_first = (jnp.cumsum(padded) - padded).astype(jnp.int32)
    first_pair = (jnp.cumsum(counts) - counts).astype(jnp.int32)
    sort_order = jnp.argsort(flat_expert, stable=True).astype(jnp.int32)
    sorted_expert = flat_expert[sort_order]
    position = padded_first[sorted_expert] + jnp.arange(pair_count, dtype=jnp.int32) - first_pair[sorted_expert]
    length_all = pair_count + EXPERTS * pad_unit
    slot_pair = jnp.full((length_all,), -1, jnp.int32).at[position].set(sort_order)
    block_first = jnp.arange(length_all // pad_unit, dtype=jnp.int32) * pad_unit
    inside = (padded_first[None, :] <= block_first[:, None]) & (block_first[:, None] < (padded_first + padded)[None, :])
    block_expert = jnp.sum(inside.astype(jnp.int32) * jnp.arange(EXPERTS, dtype=jnp.int32)[None, :], axis=1).astype(jnp.int32)
    projected = jnp.dot(out_grad, proj_out, preferred_element_type=jnp.float32).astype(jnp.bfloat16)
    flat_gates = gate_probs.reshape(-1)

    def add_block(sketch_sum, block_item):
        pair_ids, expert_id = block_item
        is_valid = pair_ids >= 0
        safe_ids = jnp.maximum(pair_ids, 0)
        token_index = safe_ids // TOP
        rows_in = tokens[token_index]
        gate_part = jnp.dot(rows_in, w_gate[expert_id], preferred_element_type=jnp.float32)
        up_part = jnp.dot(rows_in, w_up[expert_id], preferred_element_type=jnp.float32)
        hidden = (jax.nn.silu(gate_part) * up_part).astype(jnp.bfloat16)
        inputs_side = jnp.dot(hidden, proj_hidden, preferred_element_type=jnp.float32)
        output_side = flat_gates[safe_ids].astype(jnp.float32)[:, None] * projected[token_index].astype(jnp.float32)
        output_side = jnp.where(is_valid[:, None], output_side, jnp.zeros_like(output_side))
        outer = (output_side[:, :, None] * inputs_side[:, None, :]).reshape(pad_unit, R * R)
        return sketch_sum.at[doc_ids[token_index], expert_id].add(outer), None

    start_sum = jnp.zeros((NDOC, EXPERTS, R * R), jnp.float32)
    sketches, unused = lax.scan(add_block, start_sum, (slot_pair.reshape(-1, pad_unit), block_expert))
    return sketches
```

```python
import functools

import jax
import jax.numpy as jnp
from jax import lax
from jax.experimental import pallas as pl
from jax.experimental.pallas import tpu as pltpu
from jax.sharding import PartitionSpec as P

AXES = ("expert", "dp")
LANES = 128
MIB = 1 << 20


def place(width, first):
    rows = lax.broadcasted_iota(jnp.int32, (width, LANES), 0)
    lanes = lax.broadcasted_iota(jnp.int32, (width, LANES), 1)
    return (lanes == rows + first).astype(jnp.bfloat16)


def dot(a, b):
    return jnp.dot(a, b, preferred_element_type=jnp.float32)


def extend_kernel(rank, top, tokens, grads, proj, routes, gates, docs, out):
    width = tokens.shape[1]
    projected = dot(grads[...], proj[...]).astype(jnp.bfloat16)
    meta = dot(projected, place(rank, 0))
    meta += dot(gates[...], place(top, rank))
    meta += dot(routes[...].astype(jnp.float32).astype(jnp.bfloat16), place(top, rank + top))
    lanes = lax.broadcasted_iota(jnp.int32, meta.shape, 1)
    meta = jnp.where(lanes == rank + 2 * top, docs[...].astype(jnp.float32), meta)
    out[:, :width] = tokens[...]
    out[:, width:] = meta.astype(jnp.bfloat16)


def extend(tokens, out_grad, proj_out, routes, gate_probs, doc_ids):
    rows, width = tokens.shape
    body = functools.partial(extend_kernel, proj_out.shape[1], routes.shape[1])
    return pl.pallas_call(
        body,
        out_shape=jax.ShapeDtypeStruct((rows, width + LANES), jnp.bfloat16),
        compiler_params=pltpu.CompilerParams(vmem_limit_bytes=16 * MIB),
        name="extend_rows",
    )(tokens, out_grad, proj_out, routes, gate_probs, doc_ids.reshape(rows, 1))


def compact_kernel(count, capacity, top, rank, spans, experts, *refs):
    sources, outs = refs[:count], refs[count:]
    rows, total = sources[0].shape
    width = total - LANES
    meta = jnp.concatenate([s[:, width:] for s in sources], axis=0).astype(jnp.float32)
    lanes = lax.broadcasted_iota(jnp.int32, meta.shape, 1)
    is_route = (lanes >= rank + top) & (lanes < rank + 2 * top)
    hits = jnp.zeros(meta.shape, jnp.float32)
    for q in range(len(outs)):
        named = is_route & (meta == experts[q].astype(jnp.float32))
        hit = jnp.sum(named.astype(jnp.float32), axis=1, keepdims=True)
        hits = jnp.where(lanes == q, hit, hits)
    every = count * rows
    here = lax.broadcasted_iota(jnp.int32, (every, every), 0)
    other = lax.broadcasted_iota(jnp.int32, (every, every), 1)
    earlier = ((other < here) & (other // rows == here // rows)).astype(jnp.bfloat16)
    before = dot(earlier, hits.astype(jnp.bfloat16))
    first = (lax.broadcasted_iota(jnp.int32, meta.shape, 0) // rows * capacity).astype(jnp.float32)
    slots = jnp.where(hits > 0, before + first, -1.0).T
    spot = lax.broadcasted_iota(jnp.int32, (count * capacity, every), 0).astype(jnp.float32)
    picks = [(spot == slots[q : q + 1, :]).astype(jnp.bfloat16) for q in range(len(outs))]
    step = 4 * LANES
    by_span = {}
    for q, span in enumerate(spans):
        by_span.setdefault(span, []).append(q)
    for (start, stop), members in by_span.items():
        pick = jnp.concatenate([picks[q] for q in members], axis=0)
        for at in range(start, stop, step):
            end = min(at + step, stop)
            block = jnp.concatenate([s[:, at:end] for s in sources], axis=0)
            found = dot(pick, block).astype(jnp.bfloat16)
            for i, q in enumerate(members):
                outs[q][:, at - start : end - start] = found[
                    i * count * capacity : (i + 1) * count * capacity
                ]


def compact(sources, experts, spans, capacity, top, rank):
    count = len(sources)
    body = functools.partial(compact_kernel, count, capacity, top, rank, tuple(spans))
    size = sum(s.size for s in sources)
    return pl.pallas_call(
        body,
        out_shape=[
            jax.ShapeDtypeStruct((count * capacity, b - a), jnp.bfloat16) for a, b in spans
        ],
        in_specs=[pl.BlockSpec(memory_space=pltpu.SMEM)]
        + [pl.BlockSpec(memory_space=pltpu.VMEM)] * count,
        out_specs=[pl.BlockSpec(memory_space=pltpu.VMEM)] * len(spans),
        compiler_params=pltpu.CompilerParams(vmem_limit_bytes=24 * MIB),
        cost_estimate=pl.CostEstimate(flops=4 * 10**8, bytes_accessed=4 * size, transcendentals=0),
        name="compact_rows",
    )(jnp.stack(experts), *sources)


def sketch_kernel(spots, top, rank, steps, docs_total, expert, *refs):
    pieces = refs[: len(spots)]
    gate_w, up_w, proj, total_in, total_out, rows_at, hidden_at = refs[len(spots) :]
    width = rows_at.shape[1] - LANES
    step = pl.program_id(0)

    @pl.when(step == 0)
    def _():
        for ref, (row, column) in zip(pieces, spots):
            r, c = ref.shape
            rows_at[row : row + r, column : column + c] = ref[...]

    rows = rows_at[:, :width]
    gate_part = dot(rows, gate_w[0])
    up_part = dot(rows, up_w[0])
    hidden_at[step] = (gate_part / (1.0 + jnp.exp(-gate_part)) * up_part).astype(jnp.bfloat16)

    @pl.when(step == steps - 1)
    def _():
        tile = gate_w.shape[2]
        side = dot(hidden_at[0], proj[:tile])
        for s in range(1, steps):
            side += dot(hidden_at[s], proj[s * tile : (s + 1) * tile])
        meta = rows_at[:, width:]
        wide = meta.astype(jnp.float32)
        lanes = lax.broadcasted_iota(jnp.int32, wide.shape, 1)
        is_route = (lanes >= rank + top) & (lanes < rank + 2 * top)
        named = (is_route & (wide == expert[0].astype(jnp.float32))).astype(jnp.float32)
        gate = jnp.sum(wide * pltpu.roll(named, LANES - top, 1), axis=1, keepdims=True)
        spread_from = lax.broadcasted_iota(jnp.int32, (LANES, rank * rank), 0)
        spread_to = lax.broadcasted_iota(jnp.int32, (LANES, rank * rank), 1) // rank
        spread = (spread_from == spread_to).astype(jnp.bfloat16)
        output_side = dot(meta, spread) * gate
        outer = output_side * jnp.concatenate([side] * (rank * rank // LANES), axis=1)
        doc = jnp.sum(jnp.where(lanes == rank + 2 * top, wide, 0.0), axis=1, keepdims=True)
        ids = lax.broadcasted_iota(jnp.int32, (wide.shape[0], docs_total), 1).astype(jnp.float32)
        table = (ids == doc).astype(jnp.bfloat16)
        high = outer.astype(jnp.bfloat16)
        low = (outer - high.astype(jnp.float32)).astype(jnp.bfloat16)
        over_rows = (((0,), (0,)), ((), ()))
        total = total_in[...]
        for part in (high, low):
            total += lax.dot_general(table, part, over_rows, preferred_element_type=jnp.float32)
        total_out[...] = total


def sketch(pieces, spots, rows, expert, w_gate, w_up, proj_wide, total, top, rank):
    width, hidden = w_gate.shape[1:]
    tile = 256
    steps = hidden // tile
    body = functools.partial(sketch_kernel, tuple(spots), top, rank, steps, total.shape[0])
    whole = lambda a: pl.BlockSpec(a.shape, lambda i: (0,) * a.ndim)
    return pl.pallas_call(
        body,
        grid=(steps,),
        out_shape=jax.ShapeDtypeStruct(total.shape, jnp.float32),
        in_specs=[pl.BlockSpec(memory_space=pltpu.SMEM)]
        + [whole(p) for p in pieces]
        + [pl.BlockSpec((1, width, tile), lambda i: (0, 0, i))] * 2
        + [whole(proj_wide), whole(total)],
        out_specs=whole(total),
        scratch_shapes=[
            pltpu.VMEM((rows, width + LANES), jnp.bfloat16),
            pltpu.VMEM((steps, rows, tile), jnp.bfloat16),
        ],
        compiler_params=pltpu.CompilerParams(vmem_limit_bytes=40 * MIB),
        cost_estimate=pl.CostEstimate(
            flops=4 * rows * width * hidden,
            bytes_accessed=4 * width * hidden,
            transcendentals=rows * hidden,
        ),
        name="sketch_rows",
    )(expert, *pieces, w_gate, w_up, proj_wide, total)


def on_device(tokens, out_grad, routes, gate_probs, doc_ids, w_gate, w_up, proj_hidden, proj_out):
    groups, planes = lax.axis_size("expert"), lax.axis_size("dp")
    devices = groups * planes
    row_count, width = tokens.shape
    top = routes.shape[1]
    rank = proj_out.shape[1]
    capacity = max(2, 3 * row_count * top // (2 * devices))
    me = lax.axis_index(AXES).astype(jnp.int32)

    def swap(value, bits):
        return lax.ppermute(value, AXES, [(i, i ^ bits) for i in range(devices)])

    def turn(value, by):
        pairs = [(((g + by) % groups, p), (g, p)) for g in range(groups) for p in range(planes)]
        return lax.ppermute(
            value, AXES, [(a * planes + b, c * planes + d) for (a, b), (c, d) in pairs]
        )

    ext = extend(tokens, out_grad, proj_out, routes, gate_probs, doc_ids)
    order = sorted(range(groups), key=lambda j: min(j, groups - j))
    slots = [ext if j == 0 else turn(ext, j) for j in order]
    bits = [1 << b for b in range(1, planes.bit_length() - 1)]
    last = sum(bits)
    columns = {0: slots}
    for mask in sorted(range(2, last, 2), key=lambda m: bin(m).count("1")):
        low = mask & -mask
        columns[mask] = [swap(s, low) for s in columns[mask ^ low]]

    tiles = (width + LANES) // LANES
    cuts = [LANES * (tiles * i // len(bits)) for i in range(len(bits) + 1)]
    full = (0, width + LANES)
    span_of = {last ^ b: (cuts[i], cuts[i + 1]) for i, b in enumerate(bits)}
    half = groups * capacity
    args = (capacity, top, rank)
    proj_wide = jnp.tile(proj_hidden, (1, LANES // rank))
    total = jnp.zeros((devices, rank * rank), jnp.float32)
    own = me.reshape(1)
    far, far_spots = [], []

    for mask in columns:
        experts, spans = [me, me ^ 1], [full, full]
        if mask in span_of:
            hop = last ^ mask
            experts += [me ^ hop, me ^ hop ^ 1]
            spans += [span_of[mask]] * 2
        found = compact(columns[mask], experts, spans, *args)
        if mask in span_of:
            far += [swap(found[2], hop), swap(found[3], hop ^ 1)]
            far_spots += [(0, span_of[mask][0]), (half, span_of[mask][0])]
        pieces = [found[0], swap(found[1], 1)]
        spots = [(0, 0), (half, 0)]
        total = sketch(pieces, spots, 2 * half, own, w_gate, w_up, proj_wide, total, top, rank)
    total = sketch(far, far_spots, 2 * half, own, w_gate, w_up, proj_wide, total, top, rank)
    owned = lax.all_to_all(total, AXES, split_axis=0, concat_axis=0, tiled=True)
    return owned[None]


def solution(mesh):
    placed = (
        P(AXES, None),
        P(AXES, None),
        P(AXES, None),
        P(AXES, None),
        P(AXES),
        P(AXES, None, None),
        P(AXES, None, None),
        P(),
        P(),
    )
    return jax.shard_map(
        on_device,
        mesh=mesh,
        in_specs=placed,
        out_specs=P(AXES, None, None),
        check_vma=False,
    )
```

```python
import functools

import jax
import jax.numpy as jnp
from jax import lax
from jax.experimental import pallas as pl
from jax.experimental.pallas import tpu as pltpu
from jax.sharding import PartitionSpec as P

AXES = ("expert", "dp")
LANES = 128
MIB = 1 << 20


def place(width, first):
    rows = lax.broadcasted_iota(jnp.int32, (width, LANES), 0)
    lanes = lax.broadcasted_iota(jnp.int32, (width, LANES), 1)
    return (lanes == rows + first).astype(jnp.bfloat16)


def dot(a, b):
    return jnp.dot(a, b, preferred_element_type=jnp.float32)


def across(a, b, over):
    return lax.dot_general(a, b, ((over[:1], over[1:]), ((), ())), preferred_element_type=jnp.float32)


def extend_kernel(rank, top, tokens, grads, proj, routes, gates, docs, out):
    width = tokens.shape[1]
    small = jnp.float32
    projected = across(grads[...], proj[...], (1, 1)).astype(jnp.bfloat16)
    meta = dot(projected, place(rank, 0))
    meta += across(gates[...], place(top, rank), (0, 0))
    meta += across(routes[...].astype(small).astype(jnp.bfloat16), place(top, rank + top), (0, 0))
    doc = jnp.concatenate([docs[...].astype(small)] * 8, axis=0).astype(jnp.bfloat16)
    meta += across(doc, place(8, rank + 2 * top), (0, 0))
    out[:, :width] = tokens[...]
    out[:, width:] = meta.astype(jnp.bfloat16)


def extend(tokens, out_grad, proj_out, routes, gate_probs, doc_ids):
    rows, width = tokens.shape
    body = functools.partial(extend_kernel, proj_out.shape[1], routes.shape[1])
    return pl.pallas_call(
        body,
        out_shape=jax.ShapeDtypeStruct((rows, width + LANES), jnp.bfloat16),
        compiler_params=pltpu.CompilerParams(vmem_limit_bytes=16 * MIB),
        name="extend_rows",
    )(tokens, out_grad, proj_out.T, routes.T, gate_probs.T, doc_ids.reshape(1, rows))


def compact_kernel(capacity, top, rank, spans, parts, experts, after, *refs):
    count = len(refs) - len(parts)
    sources, outs = refs[:count], refs[count:]
    rows, total = sources[0].shape
    width = total - LANES
    meta = jnp.concatenate([s[:, width:] for s in sources], axis=0).astype(jnp.float32)
    lanes = lax.broadcasted_iota(jnp.int32, meta.shape, 1)
    is_route = (lanes >= rank + top) & (lanes < rank + 2 * top)
    named_by = sorted({q for members in parts for q in members})
    hits = jnp.zeros(meta.shape, jnp.float32)
    for q in named_by:
        named = is_route & (meta == experts[q].astype(jnp.float32))
        hit = jnp.sum(named.astype(jnp.float32), axis=1, keepdims=True)
        hits = jnp.where(lanes == q, hit, hits)
    every = count * rows
    here = lax.broadcasted_iota(jnp.int32, (every, every), 0)
    other = lax.broadcasted_iota(jnp.int32, (every, every), 1)
    earlier = ((other < here) & (other // rows == here // rows)).astype(jnp.bfloat16)
    before = dot(earlier, hits.astype(jnp.bfloat16))
    first = (lax.broadcasted_iota(jnp.int32, meta.shape, 0) // rows * capacity).astype(jnp.float32)
    slots = jnp.where(hits > 0, before + first, -1.0).T
    step = 4 * LANES
    for out, members, (low, high, start, stop) in zip(outs, parts, spans):
        picked = (high - low) * capacity
        spot = lax.broadcasted_iota(jnp.int32, (picked, (high - low) * rows), 0) + low * capacity
        spot = spot.astype(jnp.float32)
        pick = jnp.concatenate(
            [
                (spot == slots[q : q + 1, low * rows : high * rows]).astype(jnp.bfloat16)
                for q in members
            ],
            axis=0,
        )
        for at in range(start, stop, step):
            end = min(at + step, stop)
            block = jnp.concatenate([s[:, at:end] for s in sources[low:high]], axis=0)
            found = dot(pick, block)
            for i in range(len(members)):
                out[i, :, at - start : end - start] = found[
                    i * picked : (i + 1) * picked
                ].astype(jnp.bfloat16)


def compact(sources, experts, parts, spans, after, capacity, top, rank):
    body = functools.partial(compact_kernel, capacity, top, rank, tuple(spans), tuple(parts))
    size = sum(s.size for s in sources)
    shapes = [
        jax.ShapeDtypeStruct((len(p), (high - low) * capacity, stop - start), jnp.bfloat16)
        for p, (low, high, start, stop) in zip(parts, spans)
    ]
    return pl.pallas_call(
        body,
        out_shape=shapes,
        in_specs=[pl.BlockSpec(memory_space=pltpu.SMEM)]
        + [pl.BlockSpec(memory_space=pltpu.VMEM)] * (1 + len(sources)),
        out_specs=[pl.BlockSpec(memory_space=pltpu.VMEM)] * len(parts),
        compiler_params=pltpu.CompilerParams(vmem_limit_bytes=16 * MIB),
        cost_estimate=pl.CostEstimate(flops=4 * 10**8, bytes_accessed=4 * size, transcendentals=0),
        name="compact_rows",
    )(experts, after, *sources)


def hold_kernel(gate_w, up_w, gate_out, up_out, done, sems):
    copies = [
        pltpu.make_async_copy(gate_w.at[0], gate_out, sems.at[0]),
        pltpu.make_async_copy(up_w.at[0], up_out, sems.at[1]),
    ]
    for copy in copies:
        copy.start()
    for copy in copies:
        copy.wait()
    done[...] = jnp.zeros_like(done)


def hold(w_gate, w_up):
    shape = w_gate.shape[1:]
    return pl.pallas_call(
        hold_kernel,
        out_shape=[pltpu.VMEM(shape, jnp.bfloat16)] * 2
        + [jax.ShapeDtypeStruct((8, LANES), jnp.float32)],
        in_specs=[pl.BlockSpec(memory_space=pltpu.HBM)] * 2,
        out_specs=[pl.BlockSpec(memory_space=pltpu.VMEM)] * 3,
        scratch_shapes=[pltpu.SemaphoreType.DMA((2,))],
        compiler_params=pltpu.CompilerParams(vmem_limit_bytes=2 * MIB),
        cost_estimate=pl.CostEstimate(flops=0, bytes_accessed=16 * MIB, transcendentals=0),
        name="hold_weights",
    )(*[pltpu.with_memory_space_constraint(w, pltpu.HBM) for w in (w_gate, w_up)])


def sketch_kernel(spots, top, rank, docs_total, expert, *refs):
    pieces = refs[: len(spots)]
    gate_w, up_w, proj, total_in, total_out, rows_at, hidden_at = refs[len(spots) :]
    width, hidden = gate_w.shape
    for ref, (lead, row, column) in zip(pieces, spots):
        r, c = ref.shape[1:]
        if r % 16:
            below = row + r // 16 * 16
            rows_at[below : below + 16, column : column + c] = jnp.zeros((16, c), jnp.bfloat16)
        rows_at[row : row + r, column : column + c] = ref[lead]

    rows = rows_at[:, :width]
    tile = 256
    for at in range(0, hidden, tile):
        gate_part = dot(rows, gate_w[:, at : at + tile])
        up_part = dot(rows, up_w[:, at : at + tile])
        value = gate_part / (1.0 + jnp.exp(-gate_part)) * up_part
        hidden_at[:, at : at + tile] = value.astype(jnp.bfloat16)

    wide_proj = jnp.concatenate([proj[...]] * (LANES // rank), axis=0)
    side = across(hidden_at[...], wide_proj, (1, 1))
    meta = rows_at[:, width:]
    wide = meta.astype(jnp.float32)
    lanes = lax.broadcasted_iota(jnp.int32, wide.shape, 1)
    is_route = (lanes >= rank + top) & (lanes < rank + 2 * top)
    named = (is_route & (wide == expert[0].astype(jnp.float32))).astype(jnp.float32)
    gate = jnp.sum(wide * pltpu.roll(named, LANES - top, 1), axis=1, keepdims=True)
    spread_from = lax.broadcasted_iota(jnp.int32, (LANES, rank * rank), 0)
    spread_to = lax.broadcasted_iota(jnp.int32, (LANES, rank * rank), 1) // rank
    spread = (spread_from == spread_to).astype(jnp.bfloat16)
    output_side = dot(meta, spread) * gate
    outer = output_side * jnp.concatenate([side] * (rank * rank // LANES), axis=1)
    doc = jnp.sum(jnp.where(lanes == rank + 2 * top, wide, 0.0), axis=1, keepdims=True)
    ids = lax.broadcasted_iota(jnp.int32, (wide.shape[0], docs_total), 1).astype(jnp.float32)
    table = (ids == doc).astype(jnp.bfloat16)
    high = outer.astype(jnp.bfloat16)
    low = (outer - high.astype(jnp.float32)).astype(jnp.bfloat16)
    total = total_in[...]
    for part in (high, low):
        total += across(table, part, (0, 0))
    total_out[...] = total


def sketch(pieces, expert, weights, proj, total, top, rank):
    width, hidden = weights[0].shape
    rows, arrays, spots = 0, [], []
    for beside in pieces:
        for array, lead, column in beside:
            arrays.append(array)
            spots.append((lead, rows, column))
        rows += -(-beside[0][0].shape[1] // 16) * 16
    body = functools.partial(sketch_kernel, tuple(spots), top, rank, total.shape[0])
    vmem = pl.BlockSpec(memory_space=pltpu.VMEM)
    return pl.pallas_call(
        body,
        out_shape=jax.ShapeDtypeStruct(total.shape, jnp.float32),
        in_specs=[pl.BlockSpec(memory_space=pltpu.SMEM)] + [vmem] * (len(arrays) + 4),
        out_specs=vmem,
        scratch_shapes=[
            pltpu.VMEM((rows, width + LANES), jnp.bfloat16),
            pltpu.VMEM((rows, hidden), jnp.bfloat16),
        ],
        compiler_params=pltpu.CompilerParams(vmem_limit_bytes=20 * MIB),
        cost_estimate=pl.CostEstimate(
            flops=4 * rows * width * hidden,
            bytes_accessed=2 * rows * width,
            transcendentals=rows * hidden,
        ),
        name="sketch_rows",
    )(expert, *arrays, *weights, proj, total)


def on_device(tokens, out_grad, routes, gate_probs, doc_ids, w_gate, w_up, proj_hidden, proj_out):
    groups, planes = lax.axis_size("expert"), lax.axis_size("dp")
    devices = groups * planes
    row_count, width = tokens.shape
    top = routes.shape[1]
    rank = proj_out.shape[1]
    capacity = max(2, 3 * row_count * top // (2 * devices))
    me = lax.axis_index(AXES).astype(jnp.int32)

    def swap(value, bits):
        return lax.ppermute(value, AXES, [(i, i ^ bits) for i in range(devices)])

    def turn(value, by):
        pairs = [(((g + by) % groups, p), (g, p)) for g in range(groups) for p in range(planes)]
        return lax.ppermute(
            value, AXES, [(a * planes + b, c * planes + d) for (a, b), (c, d) in pairs]
        )

    ext = extend(tokens, out_grad, proj_out, routes, gate_probs, doc_ids)
    order = sorted(range(groups), key=lambda j: min(j, groups - j))
    slots = [ext if j == 0 else turn(ext, j) for j in order]
    bits = [1 << b for b in range(1, planes.bit_length() - 1)]
    last = sum(bits)
    masks = sorted(range(2, last, 2), key=lambda m: bin(m).count("1"))
    ends = [i for i, m in enumerate(masks) if m ^ last in bits]
    hops = [last ^ masks[i] for i in ends]
    tiles = (width + LANES) // LANES
    cuts = [LANES * (tiles * i // len(bits)) for i in range(len(bits) + 1)]
    full = (0, width + LANES)
    *weights, held = hold(w_gate, w_up)
    total = jnp.zeros((devices, rank * rank), jnp.float32)
    experts = jnp.stack([me, me ^ 1] + [me ^ hop ^ b for hop in hops for b in (0, 1)])
    own = me.reshape(1)
    args = (held, capacity, top, rank)

    def add(pieces):
        return sketch(pieces, own, weights, proj_hidden.T, total, top, rank)

    phases = [range(groups - 2), [groups - 2], [groups - 1]]
    waiting = []
    for phase in phases:
        n = len(phase)
        if phase is phases[-1]:
            slots[-1], total, *early = lax.optimization_barrier((slots[-1], total, *early))
        columns = {0: [slots[i] for i in phase]}
        for mask in masks:
            low = mask & -mask
            columns[mask] = [swap(s, low) for s in columns[mask ^ low]]
        if phase is phases[-1]:
            mine = compact(slots, experts, [(0,), (1,)], [(0, groups) + full] * 2, *args)
            total = add(waiting + [[(mine[0], 0, 0)], [(swap(mine[1], 1), 0, 0)]])
            columns, total = lax.optimization_barrier((columns, total))
        parts, spans = [(0,), (1,)], [(0, n * len(masks)) + full] * 2
        for k, i in enumerate(ends):
            parts.append((2 + 2 * k, 3 + 2 * k))
            spans.append((n * i, n * i + n, cuts[k], cuts[k + 1]))
        sources = [s for mask in masks for s in columns[mask]]
        found = compact(sources, experts, parts, spans, *args)
        arrived = [swap(f, hop) for f, hop in zip(found[2:], hops)]
        beside = [swap(f, 1) for f in arrived]
        far = [
            [(f, 0, cuts[k]) for k, f in enumerate(arrived)],
            [(f, 1, cuts[k]) for k, f in enumerate(beside)],
        ]
        near = [[(found[0], 0, 0)], [(swap(found[1], 1), 0, 0)]]
        if phase is phases[-1]:
            total = add(near + far)
        else:
            total = add(waiting + near)
            if not waiting:
                early = arrived
            waiting = far
    owned = lax.all_to_all(total, AXES, split_axis=0, concat_axis=0, tiled=True)
    return owned[None]


def solution(mesh):
    placed = (
        P(AXES, None),
        P(AXES, None),
        P(AXES, None),
        P(AXES, None),
        P(AXES),
        P(AXES, None, None),
        P(AXES, None, None),
        P(),
        P(),
    )
    return jax.shard_map(
        on_device,
        mesh=mesh,
        in_specs=placed,
        out_specs=P(AXES, None, None),
        check_vma=False,
    )
```

```python
import functools

import jax
import jax.numpy as jnp
from jax import lax
from jax.experimental import pallas as pl
from jax.experimental.pallas import tpu as pltpu
from jax.sharding import PartitionSpec as P

AXES = ("expert", "dp")
LANES = 128
MIB = 1 << 20


def place(width, first):
    rows = lax.broadcasted_iota(jnp.int32, (width, LANES), 0)
    lanes = lax.broadcasted_iota(jnp.int32, (width, LANES), 1)
    return (lanes == rows + first).astype(jnp.bfloat16)


def dot(a, b):
    return jnp.dot(a, b, preferred_element_type=jnp.float32)


def across(a, b, over):
    return lax.dot_general(a, b, ((over[:1], over[1:]), ((), ())), preferred_element_type=jnp.float32)


def extend_kernel(rank, top, tokens, *refs):
    sources, out, held, sems = refs[:5], refs[5], refs[6:11], refs[11]
    width = tokens.shape[1]
    copies = [pltpu.make_async_copy(a, b, sems.at[i]) for i, (a, b) in enumerate(zip(sources, held))]
    copies.append(pltpu.make_async_copy(tokens, out.at[:, :width], sems.at[5]))
    for copy in copies:
        copy.start()
    for copy in copies:
        copy.wait()
    grads, proj, routes, gates, docs = held
    small = jnp.float32
    projected = across(grads[...], proj[...], (1, 1)).astype(jnp.bfloat16)
    meta = dot(projected, place(rank, 0))
    meta += across(gates[...], place(top, rank), (0, 0))
    meta += across(routes[...].astype(small).astype(jnp.bfloat16), place(top, rank + top), (0, 0))
    doc = jnp.concatenate([docs[...].astype(small)] * 8, axis=0).astype(jnp.bfloat16)
    meta += across(doc, place(8, rank + 2 * top), (0, 0))
    out[:, width:] = meta.astype(jnp.bfloat16)


def extend(tokens, out_grad, proj_out, routes, gate_probs, doc_ids):
    rows, width = tokens.shape
    body = functools.partial(extend_kernel, proj_out.shape[1], routes.shape[1])
    operands = [tokens, out_grad, proj_out.T, routes.T, gate_probs.T, doc_ids.reshape(1, rows)]
    return pl.pallas_call(
        body,
        out_shape=jax.ShapeDtypeStruct((rows, width + LANES), jnp.bfloat16),
        in_specs=[pl.BlockSpec(memory_space=pltpu.HBM)] * len(operands),
        out_specs=pl.BlockSpec(memory_space=pltpu.VMEM),
        scratch_shapes=[pltpu.VMEM(o.shape, o.dtype) for o in operands[1:]]
        + [pltpu.SemaphoreType.DMA((len(operands),))],
        compiler_params=pltpu.CompilerParams(vmem_limit_bytes=16 * MIB),
        name="extend_rows",
    )(*[pltpu.with_memory_space_constraint(o, pltpu.HBM) for o in operands])


def compact_kernel(capacity, top, rank, spans, parts, experts, *refs):
    count = len(refs) - len(parts)
    sources, outs = refs[:count], refs[count:]
    rows, total = sources[0].shape
    width = total - LANES
    meta = jnp.concatenate([s[:, width:] for s in sources], axis=0).astype(jnp.float32)
    lanes = lax.broadcasted_iota(jnp.int32, meta.shape, 1)
    is_route = (lanes >= rank + top) & (lanes < rank + 2 * top)
    named_by = sorted({q for members in parts for q in members})
    hits = jnp.zeros(meta.shape, jnp.float32)
    for q in named_by:
        named = is_route & (meta == experts[q].astype(jnp.float32))
        hit = jnp.sum(named.astype(jnp.float32), axis=1, keepdims=True)
        hits = jnp.where(lanes == q, hit, hits)
    every = count * rows
    here = lax.broadcasted_iota(jnp.int32, (every, every), 0)
    other = lax.broadcasted_iota(jnp.int32, (every, every), 1)
    earlier = ((other < here) & (other // rows == here // rows)).astype(jnp.bfloat16)
    before = dot(earlier, hits.astype(jnp.bfloat16))
    first = (lax.broadcasted_iota(jnp.int32, meta.shape, 0) // rows * capacity).astype(jnp.float32)
    slots = jnp.where(hits > 0, before + first, -1.0).T
    step = 4 * LANES
    for out, members, (low, high, start, stop) in zip(outs, parts, spans):
        picked = (high - low) * capacity
        spot = lax.broadcasted_iota(jnp.int32, (picked, (high - low) * rows), 0) + low * capacity
        spot = spot.astype(jnp.float32)
        pick = jnp.concatenate(
            [
                (spot == slots[q : q + 1, low * rows : high * rows]).astype(jnp.bfloat16)
                for q in members
            ],
            axis=0,
        )
        for at in range(start, stop, step):
            end = min(at + step, stop)
            block = jnp.concatenate([s[:, at:end] for s in sources[low:high]], axis=0)
            found = dot(pick, block)
            for i in range(len(members)):
                out[i, :, at - start : end - start] = found[
                    i * picked : (i + 1) * picked
                ].astype(jnp.bfloat16)


def compact(sources, experts, parts, spans, capacity, top, rank):
    body = functools.partial(compact_kernel, capacity, top, rank, tuple(spans), tuple(parts))
    size = sum(s.size for s in sources)
    shapes = [
        jax.ShapeDtypeStruct((len(p), (high - low) * capacity, stop - start), jnp.bfloat16)
        for p, (low, high, start, stop) in zip(parts, spans)
    ]
    return pl.pallas_call(
        body,
        out_shape=shapes,
        in_specs=[pl.BlockSpec(memory_space=pltpu.SMEM)]
        + [pl.BlockSpec(memory_space=pltpu.VMEM)] * len(sources),
        out_specs=[pl.BlockSpec(memory_space=pltpu.VMEM)] * len(parts),
        compiler_params=pltpu.CompilerParams(vmem_limit_bytes=16 * MIB),
        name="compact_rows",
    )(experts, *sources)


def hold_kernel(gate_w, up_w, gate_out, up_out, sems):
    copies = [
        pltpu.make_async_copy(gate_w.at[0], gate_out, sems.at[0]),
        pltpu.make_async_copy(up_w.at[0], up_out, sems.at[1]),
    ]
    for copy in copies:
        copy.start()
    for copy in copies:
        copy.wait()


def hold(w_gate, w_up):
    shape = w_gate.shape[1:]
    return pl.pallas_call(
        hold_kernel,
        out_shape=[pltpu.VMEM(shape, jnp.bfloat16)] * 2,
        in_specs=[pl.BlockSpec(memory_space=pltpu.HBM)] * 2,
        out_specs=[pl.BlockSpec(memory_space=pltpu.VMEM)] * 2,
        scratch_shapes=[pltpu.SemaphoreType.DMA((2,))],
        compiler_params=pltpu.CompilerParams(vmem_limit_bytes=2 * MIB),
        name="hold_weights",
    )(*[pltpu.with_memory_space_constraint(w, pltpu.HBM) for w in (w_gate, w_up)])


def sketch_kernel(spots, top, rank, docs_total, expert, *refs):
    pieces = refs[: len(spots)]
    gate_w, up_w, proj, total_in, total_out, rows_at, hidden_at = refs[len(spots) :]
    width, hidden = gate_w.shape
    for ref, (lead, row, column) in zip(pieces, spots):
        r, c = ref.shape[1:]
        if r % 16:
            below = row + r // 16 * 16
            rows_at[below : below + 16, column : column + c] = jnp.zeros((16, c), jnp.bfloat16)
        rows_at[row : row + r, column : column + c] = ref[lead]

    rows = rows_at[:, :width]
    tile = 256
    for at in range(0, hidden, tile):
        gate_part = dot(rows, gate_w[:, at : at + tile])
        up_part = dot(rows, up_w[:, at : at + tile])
        value = gate_part / (1.0 + jnp.exp(-gate_part)) * up_part
        hidden_at[:, at : at + tile] = value.astype(jnp.bfloat16)

    wide_proj = jnp.concatenate([proj[...]] * (LANES // rank), axis=0)
    side = across(hidden_at[...], wide_proj, (1, 1))
    meta = rows_at[:, width:]
    wide = meta.astype(jnp.float32)
    lanes = lax.broadcasted_iota(jnp.int32, wide.shape, 1)
    is_route = (lanes >= rank + top) & (lanes < rank + 2 * top)
    named = (is_route & (wide == expert[0].astype(jnp.float32))).astype(jnp.float32)
    gate = jnp.sum(wide * pltpu.roll(named, LANES - top, 1), axis=1, keepdims=True)
    spread_from = lax.broadcasted_iota(jnp.int32, (LANES, rank * rank), 0)
    spread_to = lax.broadcasted_iota(jnp.int32, (LANES, rank * rank), 1) // rank
    spread = (spread_from == spread_to).astype(jnp.bfloat16)
    output_side = dot(meta, spread) * gate
    outer = output_side * jnp.concatenate([side] * (rank * rank // LANES), axis=1)
    doc = jnp.sum(jnp.where(lanes == rank + 2 * top, wide, 0.0), axis=1, keepdims=True)
    ids = lax.broadcasted_iota(jnp.int32, (wide.shape[0], docs_total), 1).astype(jnp.float32)
    table = (ids == doc).astype(jnp.bfloat16)
    high = outer.astype(jnp.bfloat16)
    low = (outer - high.astype(jnp.float32)).astype(jnp.bfloat16)
    total = total_in[...]
    for part in (high, low):
        total += across(table, part, (0, 0))
    total_out[...] = total


def sketch(pieces, expert, weights, proj, total, top, rank):
    width, hidden = weights[0].shape
    rows, arrays, spots = 0, [], []
    for beside in pieces:
        for array, lead, column in beside:
            arrays.append(array)
            spots.append((lead, rows, column))
        rows += -(-beside[0][0].shape[1] // 16) * 16
    body = functools.partial(sketch_kernel, tuple(spots), top, rank, total.shape[0])
    vmem = pl.BlockSpec(memory_space=pltpu.VMEM)
    return pl.pallas_call(
        body,
        out_shape=jax.ShapeDtypeStruct(total.shape, jnp.float32),
        in_specs=[pl.BlockSpec(memory_space=pltpu.SMEM)] + [vmem] * (len(arrays) + 4),
        out_specs=vmem,
        scratch_shapes=[
            pltpu.VMEM((rows, width + LANES), jnp.bfloat16),
            pltpu.VMEM((rows, hidden), jnp.bfloat16),
        ],
        compiler_params=pltpu.CompilerParams(vmem_limit_bytes=20 * MIB),
        name="sketch_rows",
    )(expert, *arrays, *weights, proj, total)


def on_device(tokens, out_grad, routes, gate_probs, doc_ids, w_gate, w_up, proj_hidden, proj_out):
    groups, planes = lax.axis_size("expert"), lax.axis_size("dp")
    devices = groups * planes
    row_count, width = tokens.shape
    top = routes.shape[1]
    rank = proj_out.shape[1]
    capacity = max(2, 3 * row_count * top // (2 * devices))
    me = lax.axis_index(AXES).astype(jnp.int32)

    def swap(value, bits):
        return lax.ppermute(value, AXES, [(i, i ^ bits) for i in range(devices)])

    def turn(value, by):
        pairs = [(((g + by) % groups, p), (g, p)) for g in range(groups) for p in range(planes)]
        return lax.ppermute(
            value, AXES, [(a * planes + b, c * planes + d) for (a, b), (c, d) in pairs]
        )

    ext = extend(tokens, out_grad, proj_out, routes, gate_probs, doc_ids)
    slots = [ext]
    for j in range(1, groups):
        slots.append(turn(slots[-1], 1))
    bits = [1 << b for b in range(1, planes.bit_length() - 1)]
    last = sum(bits)
    masks = sorted(range(2, last, 2), key=lambda m: bin(m).count("1"))
    ends = [i for i, m in enumerate(masks) if m ^ last in bits]
    hops = [last ^ masks[i] for i in ends]
    tiles = (width + LANES) // LANES
    cuts = [LANES * (tiles * i // len(bits)) for i in range(len(bits) + 1)]
    full = (0, width + LANES)
    weights = hold(w_gate, w_up)
    total = jnp.zeros((devices, rank * rank), jnp.float32)
    experts = jnp.stack([me, me ^ 1] + [me ^ hop ^ b for hop in hops for b in (0, 1)])
    own = me.reshape(1)
    args = (capacity, top, rank)

    def add(pieces):
        return sketch(pieces, own, weights, proj_hidden.T, total, top, rank)

    def halves(arrived):
        beside = [swap(f, 1) for f in arrived]
        return [[(f, 0, cut) for f, cut in zip(arrived, cuts)]] + [
            [(f, 1, cut) for f, cut in zip(beside, cuts)]
        ]

    def lanes(found):
        return [[(found[0], 0, 0)], [(swap(found[1], 1), 0, 0)]]

    def column(i):
        slot = slots[i]
        got = {0: slot}
        for mask in masks:
            low = mask & -mask
            got[mask] = swap(got[mask ^ low], low)
        return [got[mask] for mask in masks]

    def gather(sets):
        n = len(sets)
        parts, spans = [(0,), (1,)], [(0, n * len(masks)) + full] * 2
        for k, i in enumerate(ends):
            parts.append((2 + 2 * k, 3 + 2 * k))
            spans.append((n * i, n * i + n, cuts[k], cuts[k + 1]))
        sources = [s[m] for m in range(len(masks)) for s in sets]
        found = compact(sources, experts, parts, spans, *args)
        return found[:2], found[2:]

    def send(found):
        return [swap(f, hop) for f, hop in zip(found, hops)]

    columns = [column(i) for i in range(groups - 2)]
    near, far = gather(columns)
    total = add(lanes(near))
    slots[-1], far_first, total = lax.optimization_barrier((slots[-1], far, total))
    far_first = send(far_first)
    middle, total = lax.optimization_barrier((column(groups - 2), total))
    near, far = gather([middle])
    far_middle = send(far)
    mine = compact(slots, experts, [(0,), (1,)], [(0, groups) + full] * 2, *args)
    total = add(lanes(near) + lanes(mine))
    final, total = lax.optimization_barrier((column(groups - 1), total))
    near, far = gather([final])
    far_last = send(far)
    total = add(lanes(near) + halves(far_first))
    far_last, total = lax.optimization_barrier((far_last, total))
    total = add(halves(far_middle) + halves(far_last))
    owned = lax.all_to_all(total, AXES, split_axis=0, concat_axis=0, tiled=True)
    return owned[None]


def solution(mesh):
    placed = (
        P(AXES, None),
        P(AXES, None),
        P(AXES, None),
        P(AXES, None),
        P(AXES),
        P(AXES, None, None),
        P(AXES, None, None),
        P(),
        P(),
    )
    return jax.shard_map(
        on_device,
        mesh=mesh,
        in_specs=placed,
        out_specs=P(AXES, None, None),
        check_vma=False,
    )
```

```python
import functools

import jax
import jax.numpy as jnp
from jax import lax
from jax.experimental import pallas as pl
from jax.experimental.pallas import tpu as pltpu
from jax.sharding import PartitionSpec as P

AXES = ("expert", "dp")
LANES = 128
MIB = 1 << 20


def place(width, first):
    rows = lax.broadcasted_iota(jnp.int32, (width, LANES), 0)
    lanes = lax.broadcasted_iota(jnp.int32, (width, LANES), 1)
    return (lanes == rows + first).astype(jnp.bfloat16)


def dot(a, b):
    return jnp.dot(a, b, preferred_element_type=jnp.float32)


def across(a, b, over):
    return lax.dot_general(a, b, ((over[:1], over[1:]), ((), ())), preferred_element_type=jnp.float32)


def extend_kernel(rank, top, tokens, *refs):
    sources, out, held, sems = refs[:5], refs[5], refs[6:11], refs[11]
    width = tokens.shape[1]
    copies = [pltpu.make_async_copy(a, b, sems.at[i]) for i, (a, b) in enumerate(zip(sources, held))]
    copies.append(pltpu.make_async_copy(tokens, out.at[:, :width], sems.at[5]))
    for copy in copies:
        copy.start()
    for copy in copies:
        copy.wait()
    grads, proj, routes, gates, docs = held
    small = jnp.float32
    projected = across(grads[...], proj[...], (1, 1)).astype(jnp.bfloat16)
    meta = dot(projected, place(rank, 0))
    meta += across(gates[...], place(top, rank), (0, 0))
    meta += across(routes[...].astype(small).astype(jnp.bfloat16), place(top, rank + top), (0, 0))
    doc = jnp.concatenate([docs[...].astype(small)] * 8, axis=0).astype(jnp.bfloat16)
    meta += across(doc, place(8, rank + 2 * top), (0, 0))
    out[:, width:] = meta.astype(jnp.bfloat16)


def extend(tokens, out_grad, proj_out, routes, gate_probs, doc_ids):
    rows, width = tokens.shape
    body = functools.partial(extend_kernel, proj_out.shape[1], routes.shape[1])
    operands = [tokens, out_grad, proj_out.T, routes.T, gate_probs.T, doc_ids.reshape(1, rows)]
    return pl.pallas_call(
        body,
        out_shape=jax.ShapeDtypeStruct((rows, width + LANES), jnp.bfloat16),
        in_specs=[pl.BlockSpec(memory_space=pltpu.HBM)] * len(operands),
        out_specs=pl.BlockSpec(memory_space=pltpu.VMEM),
        scratch_shapes=[pltpu.VMEM(o.shape, o.dtype) for o in operands[1:]]
        + [pltpu.SemaphoreType.DMA((len(operands),))],
        compiler_params=pltpu.CompilerParams(vmem_limit_bytes=16 * MIB),
        name="extend_rows",
    )(*[pltpu.with_memory_space_constraint(o, pltpu.HBM) for o in operands])


def compact_kernel(capacity, top, rank, members, targets, *refs):
    parts = 2 if members is None else 3
    sources, outs = refs[:-parts], refs[-parts:]
    count = len(sources)
    rows, total = sources[0].shape
    width = total - LANES
    meta = jnp.concatenate([s[:, width:] for s in sources], axis=0).astype(jnp.float32)
    lanes = lax.broadcasted_iota(jnp.int32, meta.shape, 1)
    source = lax.broadcasted_iota(jnp.int32, meta.shape, 0) // rows
    is_route = (lanes >= rank + top) & (lanes < rank + 2 * top)
    hits = jnp.zeros(meta.shape, jnp.float32)
    for q in range(2 * parts - 2):
        named = is_route & (meta == targets[q].astype(jnp.float32))
        hit = jnp.sum(named.astype(jnp.float32), axis=1, keepdims=True)
        hits = jnp.where(lanes == q, hit, hits)
    first = source
    if members is not None:
        hits = jnp.where((lanes < 2) | (source // members == targets[4]), hits, 0.0)
        first = jnp.where(lanes < 2, source, source % members)
    every = count * rows
    here = lax.broadcasted_iota(jnp.int32, (every, every), 0)
    other = lax.broadcasted_iota(jnp.int32, (every, every), 1)
    earlier = ((other < here) & (other // rows == here // rows)).astype(jnp.bfloat16)
    before = dot(earlier, hits.astype(jnp.bfloat16))
    slots = jnp.where(hits > 0, before + (first * capacity).astype(jnp.float32), -1.0).T
    picks, spots = [], []
    for q in range(2 * parts - 2):
        picked = outs[min(q, 2)].shape[1]
        spot = lax.broadcasted_iota(jnp.int32, (picked, every), 0).astype(jnp.float32)
        picks.append((spot == slots[q : q + 1, :]).astype(jnp.bfloat16))
        spots.append((outs[min(q, 2)], max(q - 2, 0), picked))
    pick = jnp.concatenate(picks, axis=0)
    step = 4 * LANES
    for at in range(0, total, step):
        end = min(at + step, total)
        found = dot(pick, jnp.concatenate([s[:, at:end] for s in sources], axis=0))
        row = 0
        for out, lead, picked in spots:
            out[lead, :, at:end] = found[row : row + picked].astype(jnp.bfloat16)
            row += picked


def compact(sources, members, targets, capacity, top, rank):
    body = functools.partial(compact_kernel, capacity, top, rank, members)
    counts = [(1, len(sources))] * 2 + ([] if members is None else [(2, members)])
    shapes = [
        jax.ShapeDtypeStruct((lead, n * capacity, sources[0].shape[1]), jnp.bfloat16)
        for lead, n in counts
    ]
    return pl.pallas_call(
        body,
        out_shape=shapes,
        in_specs=[pl.BlockSpec(memory_space=pltpu.SMEM)]
        + [pl.BlockSpec(memory_space=pltpu.VMEM)] * len(sources),
        out_specs=[pl.BlockSpec(memory_space=pltpu.VMEM)] * len(shapes),
        compiler_params=pltpu.CompilerParams(vmem_limit_bytes=16 * MIB),
        name="compact_rows",
    )(targets, *sources)


def hold_kernel(gate_w, up_w, gate_out, up_out, sems):
    copies = [
        pltpu.make_async_copy(gate_w.at[0], gate_out, sems.at[0]),
        pltpu.make_async_copy(up_w.at[0], up_out, sems.at[1]),
    ]
    for copy in copies:
        copy.start()
    for copy in copies:
        copy.wait()


def hold(w_gate, w_up):
    shape = w_gate.shape[1:]
    return pl.pallas_call(
        hold_kernel,
        out_shape=[pltpu.VMEM(shape, jnp.bfloat16)] * 2,
        in_specs=[pl.BlockSpec(memory_space=pltpu.HBM)] * 2,
        out_specs=[pl.BlockSpec(memory_space=pltpu.VMEM)] * 2,
        scratch_shapes=[pltpu.SemaphoreType.DMA((2,))],
        compiler_params=pltpu.CompilerParams(vmem_limit_bytes=2 * MIB),
        name="hold_weights",
    )(*[pltpu.with_memory_space_constraint(w, pltpu.HBM) for w in (w_gate, w_up)])


def sketch_kernel(spots, top, rank, docs_total, expert, *refs):
    pieces = refs[: len(spots)]
    gate_w, up_w, proj, total_in, total_out, rows_at, hidden_at = refs[len(spots) :]
    width, hidden = gate_w.shape
    for ref, (lead, row, column) in zip(pieces, spots):
        r, c = ref.shape[1:]
        if r % 16:
            below = row + r // 16 * 16
            rows_at[below : below + 16, column : column + c] = jnp.zeros((16, c), jnp.bfloat16)
        rows_at[row : row + r, column : column + c] = ref[lead]

    rows = rows_at[:, :width]
    tile = 256
    for at in range(0, hidden, tile):
        gate_part = dot(rows, gate_w[:, at : at + tile])
        up_part = dot(rows, up_w[:, at : at + tile])
        value = gate_part / (1.0 + jnp.exp(-gate_part)) * up_part
        hidden_at[:, at : at + tile] = value.astype(jnp.bfloat16)

    wide_proj = jnp.concatenate([proj[...]] * (LANES // rank), axis=0)
    side = across(hidden_at[...], wide_proj, (1, 1))
    meta = rows_at[:, width:]
    wide = meta.astype(jnp.float32)
    lanes = lax.broadcasted_iota(jnp.int32, wide.shape, 1)
    is_route = (lanes >= rank + top) & (lanes < rank + 2 * top)
    named = (is_route & (wide == expert[0].astype(jnp.float32))).astype(jnp.float32)
    gate = jnp.sum(wide * pltpu.roll(named, LANES - top, 1), axis=1, keepdims=True)
    spread_from = lax.broadcasted_iota(jnp.int32, (LANES, rank * rank), 0)
    spread_to = lax.broadcasted_iota(jnp.int32, (LANES, rank * rank), 1) // rank
    spread = (spread_from == spread_to).astype(jnp.bfloat16)
    output_side = dot(meta, spread) * gate
    outer = output_side * jnp.concatenate([side] * (rank * rank // LANES), axis=1)
    doc = jnp.sum(jnp.where(lanes == rank + 2 * top, wide, 0.0), axis=1, keepdims=True)
    ids = lax.broadcasted_iota(jnp.int32, (wide.shape[0], docs_total), 1).astype(jnp.float32)
    table = (ids == doc).astype(jnp.bfloat16)
    high = outer.astype(jnp.bfloat16)
    low = (outer - high.astype(jnp.float32)).astype(jnp.bfloat16)
    total = total_in[...]
    for part in (high, low):
        total += across(table, part, (0, 0))
    total_out[...] = total


def sketch(pieces, expert, weights, proj, total, top, rank):
    width, hidden = weights[0].shape
    rows, arrays, spots = 0, [], []
    for beside in pieces:
        for array, lead, column in beside:
            arrays.append(array)
            spots.append((lead, rows, column))
        rows += -(-beside[0][0].shape[1] // 16) * 16
    body = functools.partial(sketch_kernel, tuple(spots), top, rank, total.shape[0])
    vmem = pl.BlockSpec(memory_space=pltpu.VMEM)
    return pl.pallas_call(
        body,
        out_shape=jax.ShapeDtypeStruct(total.shape, jnp.float32),
        in_specs=[pl.BlockSpec(memory_space=pltpu.SMEM)] + [vmem] * (len(arrays) + 4),
        out_specs=vmem,
        scratch_shapes=[
            pltpu.VMEM((rows, width + LANES), jnp.bfloat16),
            pltpu.VMEM((rows, hidden), jnp.bfloat16),
        ],
        compiler_params=pltpu.CompilerParams(vmem_limit_bytes=20 * MIB),
        name="sketch_rows",
    )(expert, *arrays, *weights, proj, total)


def on_device(tokens, out_grad, routes, gate_probs, doc_ids, w_gate, w_up, proj_hidden, proj_out):
    groups, planes = lax.axis_size("expert"), lax.axis_size("dp")
    devices = groups * planes
    row_count, width = tokens.shape
    top = routes.shape[1]
    rank = proj_out.shape[1]
    capacity = max(2, 3 * row_count * top // (2 * devices))
    me = lax.axis_index(AXES).astype(jnp.int32)

    def swap(value, bits):
        return lax.ppermute(value, AXES, [(i, i ^ bits) for i in range(devices)])

    def turn(value, by):
        pairs = [(((g + by) % groups, p), (g, p)) for g in range(groups) for p in range(planes)]
        return lax.ppermute(
            value, AXES, [(a * planes + b, c * planes + d) for (a, b), (c, d) in pairs]
        )

    ext = extend(tokens, out_grad, proj_out, routes, gate_probs, doc_ids)
    slots = [ext]
    for j in range(1, groups):
        slots.append(turn(slots[-1], 1))
    bits = [1 << b for b in range(1, planes.bit_length() - 1)]
    last = sum(bits)
    masks = sorted(range(2, last, 2), key=lambda m: bin(m).count("1"))
    side = me & 1
    hop = jnp.where(side == 0, bits[0], bits[1]).astype(jnp.int32)
    ends = [masks.index(last ^ b) for b in bits[:2]]
    chosen = jnp.where(side == 0, ends[0], ends[1]).astype(jnp.int32)
    targets = jnp.stack([me, me ^ 1, me ^ hop, me ^ hop ^ 1, chosen])
    weights = hold(w_gate, w_up)
    total = jnp.zeros((devices, rank * rank), jnp.float32)
    own = me.reshape(1)
    args = (capacity, top, rank)

    def add(pieces):
        return sketch(pieces, own, weights, proj_hidden.T, total, top, rank)

    def lanes(found):
        return [[(found[0], 0, 0)], [(swap(found[1], 1), 0, 0)]]

    def far(arrived):
        return [[(arrived, 0, 0)], [(swap(arrived, 1), 1, 0)]]

    def column(slot):
        got = {0: slot}
        for mask in masks:
            low = mask & -mask
            got[mask] = swap(got[mask ^ low], low)
        return [got[mask] for mask in masks]

    def gather(sets):
        found = compact([s[m] for m in range(len(masks)) for s in sets], len(sets), targets, *args)
        return found[:2], lax.ppermute(found[2], AXES, further)

    further = [(i, i ^ bits[i & 1]) for i in range(devices)]
    near, far_first = gather([column(slot) for slot in slots[:-2]])
    total = add(lanes(near))
    slots[-1], total = lax.optimization_barrier((slots[-1], total))
    near, far_middle = gather([column(slots[-2])])
    mine = compact(slots, None, targets, *args)
    total = add(lanes(near) + lanes(mine))
    final, total = lax.optimization_barrier((column(slots[-1]), total))
    near, far_last = gather([final])
    total = add(lanes(near) + far(far_first))
    far_last, total = lax.optimization_barrier((far_last, total))
    total = add(far(far_middle) + far(far_last))
    owned = lax.all_to_all(total, AXES, split_axis=0, concat_axis=0, tiled=True)
    return owned[None]


def solution(mesh):
    placed = (
        P(AXES, None),
        P(AXES, None),
        P(AXES, None),
        P(AXES, None),
        P(AXES),
        P(AXES, None, None),
        P(AXES, None, None),
        P(),
        P(),
    )
    return jax.shard_map(
        on_device,
        mesh=mesh,
        in_specs=placed,
        out_specs=P(AXES, None, None),
        check_vma=False,
    )
```

```python
import functools

import jax
import jax.numpy as jnp
from jax import lax
from jax.experimental import pallas as pl
from jax.experimental.pallas import tpu as pltpu
from jax.sharding import PartitionSpec as P

AXES = ("expert", "dp")
LANES = 128
MIB = 1 << 20
LIGHT = pl.CostEstimate(flops=1, bytes_accessed=1, transcendentals=0)


def place(width, first):
    rows = lax.broadcasted_iota(jnp.int32, (width, LANES), 0)
    lanes = lax.broadcasted_iota(jnp.int32, (width, LANES), 1)
    return (lanes == rows + first).astype(jnp.bfloat16)


def dot(a, b):
    return jnp.dot(a, b, preferred_element_type=jnp.float32)


def across(a, b, over):
    return lax.dot_general(a, b, ((over[:1], over[1:]), ((), ())), preferred_element_type=jnp.float32)


def extend_kernel(rank, top, tokens, *refs):
    sources, out, held, sems = refs[:5], refs[5], refs[6:11], refs[11]
    width = tokens.shape[1]
    copies = [pltpu.make_async_copy(a, b, sems.at[i]) for i, (a, b) in enumerate(zip(sources, held))]
    copies.append(pltpu.make_async_copy(tokens, out.at[:, :width], sems.at[5]))
    for copy in copies:
        copy.start()
    for copy in copies:
        copy.wait()
    grads, proj, routes, gates, docs = held
    small = jnp.float32
    projected = across(grads[...], proj[...], (1, 1)).astype(jnp.bfloat16)
    meta = dot(projected, place(rank, 0))
    meta += across(gates[...], place(top, rank), (0, 0))
    meta += across(routes[...].astype(small).astype(jnp.bfloat16), place(top, rank + top), (0, 0))
    doc = jnp.concatenate([docs[...].astype(small)] * 8, axis=0).astype(jnp.bfloat16)
    meta += across(doc, place(8, rank + 2 * top), (0, 0))
    out[:, width:] = meta.astype(jnp.bfloat16)


def extend(tokens, out_grad, proj_out, routes, gate_probs, doc_ids):
    rows, width = tokens.shape
    body = functools.partial(extend_kernel, proj_out.shape[1], routes.shape[1])
    operands = [tokens, out_grad, proj_out.T, routes.T, gate_probs.T, doc_ids.reshape(1, rows)]
    return pl.pallas_call(
        body,
        out_shape=jax.ShapeDtypeStruct((rows, width + LANES), jnp.bfloat16),
        in_specs=[pl.BlockSpec(memory_space=pltpu.HBM)] * len(operands),
        out_specs=pl.BlockSpec(memory_space=pltpu.VMEM),
        scratch_shapes=[pltpu.VMEM(o.shape, o.dtype) for o in operands[1:]]
        + [pltpu.SemaphoreType.DMA((len(operands),))],
        compiler_params=pltpu.CompilerParams(vmem_limit_bytes=4 * MIB),
        name="extend_rows",
    )(*[pltpu.with_memory_space_constraint(o, pltpu.HBM) for o in operands])


def compact_kernel(capacity, top, rank, targets, *refs):
    sources, outs = refs[:-3], refs[-3:]
    count = len(sources)
    rows, total = sources[0].shape
    width = total - LANES
    meta = jnp.concatenate([s[:, width:] for s in sources], axis=0).astype(jnp.float32)
    lanes = lax.broadcasted_iota(jnp.int32, meta.shape, 1)
    is_route = (lanes >= rank + top) & (lanes < rank + 2 * top)
    hits = jnp.zeros(meta.shape, jnp.float32)
    for q in range(4):
        named = is_route & (meta == targets[q].astype(jnp.float32))
        hit = jnp.sum(named.astype(jnp.float32), axis=1, keepdims=True)
        hits = jnp.where(lanes == q, hit, hits)
    every = count * rows
    here = lax.broadcasted_iota(jnp.int32, (every, every), 0)
    other = lax.broadcasted_iota(jnp.int32, (every, every), 1)
    earlier = ((other < here) & (other // rows == here // rows)).astype(jnp.bfloat16)
    before = dot(earlier, hits.astype(jnp.bfloat16))
    first = lax.broadcasted_iota(jnp.int32, meta.shape, 0) // rows * capacity
    slots = jnp.where(hits > 0, before + first.astype(jnp.float32), -1.0).T
    picked = count * capacity
    spot = lax.broadcasted_iota(jnp.int32, (picked, every), 0).astype(jnp.float32)
    pick = jnp.concatenate(
        [(spot == slots[q : q + 1, :]).astype(jnp.bfloat16) for q in range(4)], axis=0
    )
    step = 4 * LANES
    for at in range(0, total, step):
        end = min(at + step, total)
        found = dot(pick, jnp.concatenate([s[:, at:end] for s in sources], axis=0))
        for q in range(4):
            part = found[q * picked : (q + 1) * picked].astype(jnp.bfloat16)
            outs[min(q, 2)][max(q - 2, 0), :, at:end] = part


def compact(sources, targets, capacity, top, rank):
    body = functools.partial(compact_kernel, capacity, top, rank)
    rows, width = len(sources) * capacity, sources[0].shape[1]
    return pl.pallas_call(
        body,
        out_shape=[jax.ShapeDtypeStruct((n, rows, width), jnp.bfloat16) for n in (1, 1, 2)],
        in_specs=[pl.BlockSpec(memory_space=pltpu.SMEM)]
        + [pl.BlockSpec(memory_space=pltpu.VMEM)] * len(sources),
        out_specs=[pl.BlockSpec(memory_space=pltpu.VMEM)] * 3,
        compiler_params=pltpu.CompilerParams(vmem_limit_bytes=8 * MIB),
        cost_estimate=LIGHT,
        name="compact_rows",
    )(targets, *sources)


def hold_kernel(gate_w, up_w, gate_out, up_out, sems):
    copies = [
        pltpu.make_async_copy(gate_w.at[0], gate_out, sems.at[0]),
        pltpu.make_async_copy(up_w.at[0], up_out, sems.at[1]),
    ]
    for copy in copies:
        copy.start()
    for copy in copies:
        copy.wait()


def hold(w_gate, w_up):
    shape = w_gate.shape[1:]
    return pl.pallas_call(
        hold_kernel,
        out_shape=[pltpu.VMEM(shape, jnp.bfloat16)] * 2,
        in_specs=[pl.BlockSpec(memory_space=pltpu.HBM)] * 2,
        out_specs=[pl.BlockSpec(memory_space=pltpu.VMEM)] * 2,
        scratch_shapes=[pltpu.SemaphoreType.DMA((2,))],
        compiler_params=pltpu.CompilerParams(vmem_limit_bytes=2 * MIB),
        cost_estimate=LIGHT,
        name="hold_weights",
    )(*[pltpu.with_memory_space_constraint(w, pltpu.HBM) for w in (w_gate, w_up)])


def sketch_kernel(spots, top, rank, docs_total, expert, *refs):
    pieces = refs[: len(spots)]
    gate_w, up_w, proj, total_in, total_out, rows_at, hidden_at = refs[len(spots) :]
    width, hidden = gate_w.shape
    for ref, (lead, row, column) in zip(pieces, spots):
        r, c = ref.shape[1:]
        if r % 16:
            below = row + r // 16 * 16
            rows_at[below : below + 16, column : column + c] = jnp.zeros((16, c), jnp.bfloat16)
        rows_at[row : row + r, column : column + c] = ref[lead]

    rows = rows_at[:, :width]
    tile = 256
    for at in range(0, hidden, tile):
        gate_part = dot(rows, gate_w[:, at : at + tile])
        up_part = dot(rows, up_w[:, at : at + tile])
        value = gate_part / (1.0 + jnp.exp(-gate_part)) * up_part
        hidden_at[:, at : at + tile] = value.astype(jnp.bfloat16)

    wide_proj = jnp.concatenate([proj[...]] * (LANES // rank), axis=0)
    side = across(hidden_at[...], wide_proj, (1, 1))
    meta = rows_at[:, width:]
    wide = meta.astype(jnp.float32)
    lanes = lax.broadcasted_iota(jnp.int32, wide.shape, 1)
    is_route = (lanes >= rank + top) & (lanes < rank + 2 * top)
    named = (is_route & (wide == expert[0].astype(jnp.float32))).astype(jnp.float32)
    gate = jnp.sum(wide * pltpu.roll(named, LANES - top, 1), axis=1, keepdims=True)
    spread_from = lax.broadcasted_iota(jnp.int32, (LANES, rank * rank), 0)
    spread_to = lax.broadcasted_iota(jnp.int32, (LANES, rank * rank), 1) // rank
    spread = (spread_from == spread_to).astype(jnp.bfloat16)
    output_side = dot(meta, spread) * gate
    outer = output_side * jnp.concatenate([side] * (rank * rank // LANES), axis=1)
    doc = jnp.sum(jnp.where(lanes == rank + 2 * top, wide, 0.0), axis=1, keepdims=True)
    ids = lax.broadcasted_iota(jnp.int32, (wide.shape[0], docs_total), 1).astype(jnp.float32)
    table = (ids == doc).astype(jnp.bfloat16)
    high = outer.astype(jnp.bfloat16)
    low = (outer - high.astype(jnp.float32)).astype(jnp.bfloat16)
    total = total_in[...]
    for part in (high, low):
        total += across(table, part, (0, 0))
    total_out[...] = total


def sketch(pieces, expert, weights, proj, total, top, rank):
    width, hidden = weights[0].shape
    rows, arrays, spots = 0, [], []
    for beside in pieces:
        for array, lead, column in beside:
            arrays.append(array)
            spots.append((lead, rows, column))
        rows += -(-beside[0][0].shape[1] // 16) * 16
    body = functools.partial(sketch_kernel, tuple(spots), top, rank, total.shape[0])
    vmem = pl.BlockSpec(memory_space=pltpu.VMEM)
    return pl.pallas_call(
        body,
        out_shape=jax.ShapeDtypeStruct(total.shape, jnp.float32),
        in_specs=[pl.BlockSpec(memory_space=pltpu.SMEM)] + [vmem] * (len(arrays) + 4),
        out_specs=vmem,
        scratch_shapes=[
            pltpu.VMEM((rows, width + LANES), jnp.bfloat16),
            pltpu.VMEM((rows, hidden), jnp.bfloat16),
        ],
        compiler_params=pltpu.CompilerParams(vmem_limit_bytes=14 * MIB),
        cost_estimate=LIGHT,
        name="sketch_rows",
    )(expert, *arrays, *weights, proj, total)


def on_device(tokens, out_grad, routes, gate_probs, doc_ids, w_gate, w_up, proj_hidden, proj_out):
    groups, planes = lax.axis_size("expert"), lax.axis_size("dp")
    devices = groups * planes
    row_count, width = tokens.shape
    top = routes.shape[1]
    rank = proj_out.shape[1]
    capacity = max(2, 3 * row_count * top // (2 * devices))
    me = lax.axis_index(AXES).astype(jnp.int32)

    def swap(value, hops):
        return lax.ppermute(value, AXES, [(i, i ^ hops[i & 1]) for i in range(devices)])

    def turn(value, by):
        pairs = [(((g + by) % groups, p), (g, p)) for g in range(groups) for p in range(planes)]
        return lax.ppermute(
            value, AXES, [(a * planes + b, c * planes + d) for (a, b), (c, d) in pairs]
        )

    ext = extend(tokens, out_grad, proj_out, routes, gate_probs, doc_ids)
    slots = [ext]
    for j in range(1, groups - 1):
        slots.append(turn(slots[-1], 1))
    slots.insert(groups - 2, turn(ext, groups - 1))
    bits = [1 << b for b in range(1, planes.bit_length() - 1)]
    shared = [[b for b in bits if b != bits[core]] for core in (0, 1)]
    side = jnp.where(me & 1 == 0, bits[0], bits[1]).astype(jnp.int32)
    targets = jnp.stack([me, me ^ 1, me ^ side, me ^ side ^ 1])
    weights = hold(w_gate, w_up)
    total = jnp.zeros((devices, rank * rank), jnp.float32)
    own = me.reshape(1)
    args = (capacity, top, rank)

    def sketch_of(total, pieces):
        return sketch(pieces, own, weights, proj_hidden.T, total, top, rank)

    def gather(slot):
        sources = [slot]
        for hops in zip(*shared):
            sources += [swap(s, hops) for s in sources]
        return sources

    def spread(sources):
        own, other, further = compact(sources, targets, *args)
        return [own, swap(other, (1, 1))], swap(further, bits)

    def near(*pairs):
        return [[(array, 0, 0)] for pair in pairs for array in pair]

    def far(*arrays):
        return [
            [piece] for a in arrays for piece in ((a, 0, 0), (swap(a, (1, 1)), 1, 0))
        ]

    tied = lax.optimization_barrier
    near_now, far_now = spread(gather(slots[0]))
    near_kept, far_kept, far_now = [], [far_now], None
    for j in range(1, groups):
        sources, coming = gather(slots[j]), slots[j + 1 : j + 2]
        group = (near_now, far_kept, sources, coming, [total] if far_kept else [])
        near_now, far_kept, sources, slots[j + 1 : j + 2], kept = tied(group)
        near_kept += near_now
        near_now, far_next = spread(sources)
        if far_kept:
            total = sketch_of(kept[0], near(near_kept) + far(*far_kept))
            near_kept = []
        far_kept = [] if far_now is None else [far_now]
        far_now = far_next
    near_now, far_kept = tied((near_now, far_kept))
    total = sketch_of(total, near(near_kept, near_now) + far(*far_kept))
    far_now, total = tied((far_now, total))
    total = sketch_of(total, far(far_now))
    owned = lax.all_to_all(total, AXES, split_axis=0, concat_axis=0, tiled=True)
    return owned[None]


def solution(mesh):
    placed = (
        P(AXES, None),
        P(AXES, None),
        P(AXES, None),
        P(AXES, None),
        P(AXES),
        P(AXES, None, None),
        P(AXES, None, None),
        P(),
        P(),
    )
    return jax.shard_map(
        on_device,
        mesh=mesh,
        in_specs=placed,
        out_specs=P(AXES, None, None),
        check_vma=False,
    )
```

```python
import functools

import jax
import jax.numpy as jnp
from jax import lax
from jax.experimental import pallas as pl
from jax.experimental.pallas import tpu as pltpu
from jax.sharding import PartitionSpec as P

AXES = ("expert", "dp")
LANES = 128
MIB = 1 << 20
LIGHT = pl.CostEstimate(flops=1, bytes_accessed=1, transcendentals=0)


def place(width, first):
    rows = lax.broadcasted_iota(jnp.int32, (width, LANES), 0)
    lanes = lax.broadcasted_iota(jnp.int32, (width, LANES), 1)
    return (lanes == rows + first).astype(jnp.bfloat16)


def dot(a, b):
    return jnp.dot(a, b, preferred_element_type=jnp.float32)


def across(a, b, over):
    return lax.dot_general(a, b, ((over[:1], over[1:]), ((), ())), preferred_element_type=jnp.float32)


def extend_kernel(rank, top, tokens, *refs):
    sources, out, held, sems = refs[:5], refs[5], refs[6:11], refs[11]
    width = tokens.shape[1]
    copies = [pltpu.make_async_copy(a, b, sems.at[i]) for i, (a, b) in enumerate(zip(sources, held))]
    copies.append(pltpu.make_async_copy(tokens, out.at[:, :width], sems.at[5]))
    for copy in copies:
        copy.start()
    for copy in copies:
        copy.wait()
    grads, proj, routes, gates, docs = held
    small = jnp.float32
    projected = across(grads[...], proj[...], (1, 1)).astype(jnp.bfloat16)
    meta = dot(projected, place(rank, 0))
    meta += across(gates[...], place(top, rank), (0, 0))
    meta += across(routes[...].astype(small).astype(jnp.bfloat16), place(top, rank + top), (0, 0))
    doc = jnp.concatenate([docs[...].astype(small)] * 8, axis=0).astype(jnp.bfloat16)
    meta += across(doc, place(8, rank + 2 * top), (0, 0))
    out[:, width:] = meta.astype(jnp.bfloat16)


def extend(tokens, out_grad, proj_out, routes, gate_probs, doc_ids):
    rows, width = tokens.shape
    body = functools.partial(extend_kernel, proj_out.shape[1], routes.shape[1])
    operands = [tokens, out_grad, proj_out.T, routes.T, gate_probs.T, doc_ids.reshape(1, rows)]
    return pl.pallas_call(
        body,
        out_shape=jax.ShapeDtypeStruct((rows, width + LANES), jnp.bfloat16),
        in_specs=[pl.BlockSpec(memory_space=pltpu.HBM)] * len(operands),
        out_specs=pl.BlockSpec(memory_space=pltpu.VMEM),
        scratch_shapes=[pltpu.VMEM(o.shape, o.dtype) for o in operands[1:]]
        + [pltpu.SemaphoreType.DMA((len(operands),))],
        compiler_params=pltpu.CompilerParams(vmem_limit_bytes=4 * MIB),
        name="extend_rows",
    )(*[pltpu.with_memory_space_constraint(o, pltpu.HBM) for o in operands])


def compact_kernel(spots, capacity, top, rank, targets, after, *refs):
    parts = 1 + spots[-1][0]
    sources, outs = refs[:-parts], refs[-parts:]
    count = len(sources)
    rows, total = sources[0].shape
    width = total - LANES
    meta = jnp.concatenate([s[:, width:] for s in sources], axis=0).astype(jnp.float32)
    lanes = lax.broadcasted_iota(jnp.int32, meta.shape, 1)
    is_route = (lanes >= rank + top) & (lanes < rank + 2 * top)
    hits = jnp.zeros(meta.shape, jnp.float32)
    for q in range(4):
        named = is_route & (meta == targets[q].astype(jnp.float32))
        hit = jnp.sum(named.astype(jnp.float32), axis=1, keepdims=True)
        hits = jnp.where(lanes == q, hit, hits)
    every = count * rows
    here = lax.broadcasted_iota(jnp.int32, (every, every), 0)
    other = lax.broadcasted_iota(jnp.int32, (every, every), 1)
    earlier = ((other < here) & (other // rows == here // rows)).astype(jnp.bfloat16)
    before = dot(earlier, hits.astype(jnp.bfloat16))
    first = lax.broadcasted_iota(jnp.int32, meta.shape, 0) // rows * capacity
    slots = jnp.where(hits > 0, before + first.astype(jnp.float32), -1.0).T
    picked = count * capacity
    spot = lax.broadcasted_iota(jnp.int32, (picked, every), 0).astype(jnp.float32)
    pick = jnp.concatenate(
        [(spot == slots[q : q + 1, :]).astype(jnp.bfloat16) for q in range(4)], axis=0
    )
    step = 4 * LANES
    for at in range(0, total, step):
        end = min(at + step, total)
        found = dot(pick, jnp.concatenate([s[:, at:end] for s in sources], axis=0))
        for q, (out, lead) in enumerate(spots):
            part = found[q * picked : (q + 1) * picked].astype(jnp.bfloat16)
            outs[out][lead, :, at:end] = part


def compact(sources, targets, after, leads, capacity, top, rank):
    spots = tuple((i, lead) for i, n in enumerate(leads) for lead in range(n))
    body = functools.partial(compact_kernel, spots, capacity, top, rank)
    rows, width = len(sources) * capacity, sources[0].shape[1]
    return pl.pallas_call(
        body,
        out_shape=[jax.ShapeDtypeStruct((n, rows, width), jnp.bfloat16) for n in leads],
        in_specs=[pl.BlockSpec(memory_space=pltpu.SMEM)] * 2
        + [pl.BlockSpec(memory_space=pltpu.VMEM)] * len(sources),
        out_specs=[pl.BlockSpec(memory_space=pltpu.VMEM)] * len(leads),
        compiler_params=pltpu.CompilerParams(vmem_limit_bytes=8 * MIB),
        cost_estimate=LIGHT,
        name="compact_rows",
    )(targets, after, *sources)


def hold_kernel(gate_w, up_w, gate_out, up_out, done, sems):
    copies = [
        pltpu.make_async_copy(gate_w.at[0], gate_out, sems.at[0]),
        pltpu.make_async_copy(up_w.at[0], up_out, sems.at[1]),
    ]
    for copy in copies:
        copy.start()
    for copy in copies:
        copy.wait()
    done[0] = 0


def hold(w_gate, w_up):
    shape = w_gate.shape[1:]
    return pl.pallas_call(
        hold_kernel,
        out_shape=[pltpu.VMEM(shape, jnp.bfloat16)] * 2 + [jax.ShapeDtypeStruct((1,), jnp.int32)],
        in_specs=[pl.BlockSpec(memory_space=pltpu.HBM)] * 2,
        out_specs=[pl.BlockSpec(memory_space=pltpu.VMEM)] * 2
        + [pl.BlockSpec(memory_space=pltpu.SMEM)],
        scratch_shapes=[pltpu.SemaphoreType.DMA((2,))],
        compiler_params=pltpu.CompilerParams(vmem_limit_bytes=2 * MIB),
        cost_estimate=LIGHT,
        name="hold_weights",
    )(*[pltpu.with_memory_space_constraint(w, pltpu.HBM) for w in (w_gate, w_up)])


def sketch_kernel(spots, top, rank, docs_total, expert, *refs):
    pieces = refs[: len(spots)]
    gate_w, up_w, proj, total_in, total_out, rows_at, hidden_at = refs[len(spots) :]
    width, hidden = gate_w.shape
    for ref, (lead, row, column) in zip(pieces, spots):
        r, c = ref.shape[1:]
        if r % 16:
            below = row + r // 16 * 16
            rows_at[below : below + 16, column : column + c] = jnp.zeros((16, c), jnp.bfloat16)
        rows_at[row : row + r, column : column + c] = ref[lead]

    rows = rows_at[:, :width]
    tile = 256
    for at in range(0, hidden, tile):
        gate_part = dot(rows, gate_w[:, at : at + tile])
        up_part = dot(rows, up_w[:, at : at + tile])
        value = gate_part / (1.0 + jnp.exp(-gate_part)) * up_part
        hidden_at[:, at : at + tile] = value.astype(jnp.bfloat16)

    wide_proj = jnp.concatenate([proj[...]] * (LANES // rank), axis=0)
    side = across(hidden_at[...], wide_proj, (1, 1))
    meta = rows_at[:, width:]
    wide = meta.astype(jnp.float32)
    lanes = lax.broadcasted_iota(jnp.int32, wide.shape, 1)
    is_route = (lanes >= rank + top) & (lanes < rank + 2 * top)
    named = (is_route & (wide == expert[0].astype(jnp.float32))).astype(jnp.float32)
    gate = jnp.sum(wide * pltpu.roll(named, LANES - top, 1), axis=1, keepdims=True)
    spread_from = lax.broadcasted_iota(jnp.int32, (LANES, rank * rank), 0)
    spread_to = lax.broadcasted_iota(jnp.int32, (LANES, rank * rank), 1) // rank
    spread = (spread_from == spread_to).astype(jnp.bfloat16)
    output_side = dot(meta, spread) * gate
    outer = output_side * jnp.concatenate([side] * (rank * rank // LANES), axis=1)
    doc = jnp.sum(jnp.where(lanes == rank + 2 * top, wide, 0.0), axis=1, keepdims=True)
    ids = lax.broadcasted_iota(jnp.int32, (wide.shape[0], docs_total), 1).astype(jnp.float32)
    table = (ids == doc).astype(jnp.bfloat16)
    high = outer.astype(jnp.bfloat16)
    low = (outer - high.astype(jnp.float32)).astype(jnp.bfloat16)
    total = total_in[...]
    for part in (high, low):
        total += across(table, part, (0, 0))
    total_out[...] = total


def sketch(pieces, expert, weights, proj, total, top, rank):
    width, hidden = weights[0].shape
    rows, arrays, spots = 0, [], []
    for beside in pieces:
        for array, lead, column in beside:
            arrays.append(array)
            spots.append((lead, rows, column))
        rows += -(-beside[0][0].shape[1] // 16) * 16
    body = functools.partial(sketch_kernel, tuple(spots), top, rank, total.shape[0])
    vmem = pl.BlockSpec(memory_space=pltpu.VMEM)
    return pl.pallas_call(
        body,
        out_shape=jax.ShapeDtypeStruct(total.shape, jnp.float32),
        in_specs=[pl.BlockSpec(memory_space=pltpu.SMEM)] + [vmem] * (len(arrays) + 4),
        out_specs=vmem,
        scratch_shapes=[
            pltpu.VMEM((rows, width + LANES), jnp.bfloat16),
            pltpu.VMEM((rows, hidden), jnp.bfloat16),
        ],
        compiler_params=pltpu.CompilerParams(vmem_limit_bytes=14 * MIB),
        cost_estimate=LIGHT,
        name="sketch_rows",
    )(expert, *arrays, *weights, proj, total)


def on_device(tokens, out_grad, routes, gate_probs, doc_ids, w_gate, w_up, proj_hidden, proj_out):
    groups, planes = lax.axis_size("expert"), lax.axis_size("dp")
    devices = groups * planes
    row_count, width = tokens.shape
    top = routes.shape[1]
    rank = proj_out.shape[1]
    capacity = max(2, 3 * row_count * top // (2 * devices))
    me = lax.axis_index(AXES).astype(jnp.int32)

    def swap(value, hops):
        return lax.ppermute(value, AXES, [(i, i ^ hops[i & 1]) for i in range(devices)])

    def turn(value, by):
        pairs = [(((g + by) % groups, p), (g, p)) for g in range(groups) for p in range(planes)]
        return lax.ppermute(
            value, AXES, [(a * planes + b, c * planes + d) for (a, b), (c, d) in pairs]
        )

    ext = extend(tokens, out_grad, proj_out, routes, gate_probs, doc_ids)
    slots = [ext]
    for j in range(1, groups - 1):
        slots.append(turn(slots[-1], 1))
    slots.insert(groups - 2, turn(ext, groups - 1))
    bits = [1 << b for b in range(1, planes.bit_length() - 1)]
    shared = [[b for b in bits if b != bits[core]] for core in (0, 1)]
    side = jnp.where(me & 1 == 0, bits[0], bits[1]).astype(jnp.int32)
    targets = jnp.stack([me, me ^ 1, me ^ side, me ^ side ^ 1])
    *weights, held = hold(w_gate, w_up)
    total = jnp.zeros((devices, rank * rank), jnp.float32)
    own_id = me.reshape(1)
    args = (capacity, top, rank)

    def sketch_of(total, pieces):
        return sketch(pieces, own_id, weights, proj_hidden.T, total, top, rank)

    def gather(slot):
        sources = [slot]
        for hops in zip(*shared):
            sources += [swap(s, hops) for s in sources]
        return sources

    def spread(sources, after=own_id):
        own, other, further = compact(sources, targets, after, (1, 1, 2), *args)
        return [own, swap(other, (1, 1))], swap(further, bits)

    def spread_apart(sources):
        own, other, same, crossed = compact(sources, targets, own_id, (1, 1, 1, 1), *args)
        return [own, swap(other, (1, 1))], [swap(same, bits), swap(crossed, [b ^ 1 for b in bits])]

    def near(*pairs):
        return [[(array, 0, 0)] for pair in pairs for array in pair]

    def across_core(array):
        return [array, swap(array, (1, 1))]

    def far(*pairs):
        return [[piece] for a, b in pairs for piece in ((a, 0, 0), (b, 1, 0))]

    tied = lax.optimization_barrier
    near_now, far_now = spread(gather(slots[0]))
    near_kept, far_kept, far_now = [], [far_now], None
    for j in range(1, groups):
        sources, coming = gather(slots[j]), slots[j + 1 : j + 2]
        if j == groups - 1:
            total = sketch_of(total, near(near_kept, near_now) + far(*map(across_core, far_old)))
            near_kept, near_now = [], []
        group = (near_now, far_kept, sources, coming, [total] if j != 2 else [held])
        near_now, far_kept, sources, slots[j + 1 : j + 2], kept = tied(group)
        near_kept += near_now
        if j == groups - 1:
            near_now, far_next = spread_apart(sources)
            total = kept[0]
        else:
            near_now, far_next = spread(sources, kept[0] if j == 2 else own_id)
        if j == 1:
            far_old = far_kept
            far_kept = []
        elif far_now is not None:
            far_kept = far_kept + [far_now]
        far_now = far_next
    near_now, far_kept = tied((near_now, far_kept))
    total = sketch_of(total, near(near_kept, near_now) + far(*map(across_core, far_kept)))
    far_now, total = tied((far_now, total))
    total = sketch_of(total, near(far_now))
    owned = lax.all_to_all(total, AXES, split_axis=0, concat_axis=0, tiled=True)
    return owned[None]


def solution(mesh):
    placed = (
        P(AXES, None),
        P(AXES, None),
        P(AXES, None),
        P(AXES, None),
        P(AXES),
        P(AXES, None, None),
        P(AXES, None, None),
        P(),
        P(),
    )
    return jax.shard_map(
        on_device,
        mesh=mesh,
        in_specs=placed,
        out_specs=P(AXES, None, None),
        check_vma=False,
    )
```

```python
import functools

import jax
import jax.numpy as jnp
from jax import lax
from jax.experimental import pallas as pl
from jax.experimental.pallas import tpu as pltpu
from jax.sharding import PartitionSpec as P

AXES = ("expert", "dp")
LANES = 128
MIB = 1 << 20
LIGHT = pl.CostEstimate(flops=1, bytes_accessed=1, transcendentals=0)


def place(width, first):
    rows = lax.broadcasted_iota(jnp.int32, (width, LANES), 0)
    lanes = lax.broadcasted_iota(jnp.int32, (width, LANES), 1)
    return (lanes == rows + first).astype(jnp.bfloat16)


def dot(a, b):
    return jnp.dot(a, b, preferred_element_type=jnp.float32)


def across(a, b, over):
    return lax.dot_general(a, b, ((over[:1], over[1:]), ((), ())), preferred_element_type=jnp.float32)


def extend_kernel(rank, top, tokens, *refs):
    sources, out, held, sems = refs[:5], refs[5], refs[6:11], refs[11]
    width = tokens.shape[1]
    copies = [pltpu.make_async_copy(a, b, sems.at[i]) for i, (a, b) in enumerate(zip(sources, held))]
    copies.append(pltpu.make_async_copy(tokens, out.at[:, :width], sems.at[5]))
    for copy in copies:
        copy.start()
    for copy in copies:
        copy.wait()
    grads, proj, routes, gates, docs = held
    small = jnp.float32
    projected = across(grads[...], proj[...], (1, 1)).astype(jnp.bfloat16)
    meta = dot(projected, place(rank, 0))
    meta += across(gates[...], place(top, rank), (0, 0))
    meta += across(routes[...].astype(small).astype(jnp.bfloat16), place(top, rank + top), (0, 0))
    doc = jnp.concatenate([docs[...].astype(small)] * 8, axis=0).astype(jnp.bfloat16)
    meta += across(doc, place(8, rank + 2 * top), (0, 0))
    out[:, width:] = meta.astype(jnp.bfloat16)


def extend(tokens, out_grad, proj_out, routes, gate_probs, doc_ids):
    rows, width = tokens.shape
    body = functools.partial(extend_kernel, proj_out.shape[1], routes.shape[1])
    operands = [tokens, out_grad, proj_out.T, routes.T, gate_probs.T, doc_ids.reshape(1, rows)]
    return pl.pallas_call(
        body,
        out_shape=jax.ShapeDtypeStruct((rows, width + LANES), jnp.bfloat16),
        in_specs=[pl.BlockSpec(memory_space=pltpu.HBM)] * len(operands),
        out_specs=pl.BlockSpec(memory_space=pltpu.VMEM),
        scratch_shapes=[pltpu.VMEM(o.shape, o.dtype) for o in operands[1:]]
        + [pltpu.SemaphoreType.DMA((len(operands),))],
        compiler_params=pltpu.CompilerParams(vmem_limit_bytes=4 * MIB),
        name="extend_rows",
    )(*[pltpu.with_memory_space_constraint(o, pltpu.HBM) for o in operands])


def compact_kernel(spots, capacity, top, rank, targets, after, *refs):
    parts = 1 + spots[-1][0]
    sources, outs = refs[:-parts], refs[-parts:]
    count = len(sources)
    rows, total = sources[0].shape
    width = total - LANES
    meta = jnp.concatenate([s[:, width:] for s in sources], axis=0).astype(jnp.float32)
    lanes = lax.broadcasted_iota(jnp.int32, meta.shape, 1)
    is_route = (lanes >= rank + top) & (lanes < rank + 2 * top)
    hits = jnp.zeros(meta.shape, jnp.float32)
    for q in range(4):
        named = is_route & (meta == targets[q].astype(jnp.float32))
        hit = jnp.sum(named.astype(jnp.float32), axis=1, keepdims=True)
        hits = jnp.where(lanes == q, hit, hits)
    every = count * rows
    here = lax.broadcasted_iota(jnp.int32, (every, every), 0)
    other = lax.broadcasted_iota(jnp.int32, (every, every), 1)
    earlier = ((other < here) & (other // rows == here // rows)).astype(jnp.bfloat16)
    before = dot(earlier, hits.astype(jnp.bfloat16))
    first = lax.broadcasted_iota(jnp.int32, meta.shape, 0) // rows * capacity
    slots = jnp.where(hits > 0, before + first.astype(jnp.float32), -1.0).T
    picked = count * capacity
    spot = lax.broadcasted_iota(jnp.int32, (picked, every), 0).astype(jnp.float32)
    pick = jnp.concatenate(
        [(spot == slots[q : q + 1, :]).astype(jnp.bfloat16) for q in range(4)], axis=0
    )
    step = 4 * LANES
    for at in range(0, total, step):
        end = min(at + step, total)
        found = dot(pick, jnp.concatenate([s[:, at:end] for s in sources], axis=0))
        for q, (out, lead) in enumerate(spots):
            part = found[q * picked : (q + 1) * picked].astype(jnp.bfloat16)
            outs[out][lead, :, at:end] = part


def compact(sources, targets, after, leads, capacity, top, rank):
    spots = tuple((i, lead) for i, n in enumerate(leads) for lead in range(n))
    body = functools.partial(compact_kernel, spots, capacity, top, rank)
    rows, width = len(sources) * capacity, sources[0].shape[1]
    return pl.pallas_call(
        body,
        out_shape=[jax.ShapeDtypeStruct((n, rows, width), jnp.bfloat16) for n in leads],
        in_specs=[pl.BlockSpec(memory_space=pltpu.SMEM)] * 2
        + [pl.BlockSpec(memory_space=pltpu.VMEM)] * len(sources),
        out_specs=[pl.BlockSpec(memory_space=pltpu.VMEM)] * len(leads),
        compiler_params=pltpu.CompilerParams(vmem_limit_bytes=8 * MIB),
        cost_estimate=LIGHT,
        name="compact_rows",
    )(targets, after, *sources)


def hold_kernel(gate_w, up_w, gate_out, up_out, done, sems):
    copies = [
        pltpu.make_async_copy(gate_w.at[0], gate_out, sems.at[0]),
        pltpu.make_async_copy(up_w.at[0], up_out, sems.at[1]),
    ]
    for copy in copies:
        copy.start()
    for copy in copies:
        copy.wait()
    done[0] = 0


def hold(w_gate, w_up):
    shape = w_gate.shape[1:]
    return pl.pallas_call(
        hold_kernel,
        out_shape=[pltpu.VMEM(shape, jnp.bfloat16)] * 2 + [jax.ShapeDtypeStruct((1,), jnp.int32)],
        in_specs=[pl.BlockSpec(memory_space=pltpu.HBM)] * 2,
        out_specs=[pl.BlockSpec(memory_space=pltpu.VMEM)] * 2
        + [pl.BlockSpec(memory_space=pltpu.SMEM)],
        scratch_shapes=[pltpu.SemaphoreType.DMA((2,))],
        compiler_params=pltpu.CompilerParams(vmem_limit_bytes=2 * MIB),
        cost_estimate=LIGHT,
        name="hold_weights",
    )(*[pltpu.with_memory_space_constraint(w, pltpu.HBM) for w in (w_gate, w_up)])


def sketch_kernel(spots, top, rank, docs_total, expert, *refs):
    pieces = refs[: len(spots)]
    gate_w, up_w, proj, total_in, total_out, rows_at, hidden_at, *folded = refs[len(spots) :]
    width, hidden = gate_w.shape
    for ref, (lead, row, column) in zip(pieces, spots):
        r, c = ref.shape[1:]
        if r % 16:
            below = row + r // 16 * 16
            rows_at[below : below + 16, column : column + c] = jnp.zeros((16, c), jnp.bfloat16)
        rows_at[row : row + r, column : column + c] = ref[lead]

    rows = rows_at[:, :width]
    tile = 256
    for at in range(0, hidden, tile):
        gate_part = dot(rows, gate_w[:, at : at + tile])
        up_part = dot(rows, up_w[:, at : at + tile])
        value = gate_part / (1.0 + jnp.exp(-gate_part)) * up_part
        hidden_at[:, at : at + tile] = value.astype(jnp.bfloat16)

    wide_proj = jnp.concatenate([proj[...]] * (LANES // rank), axis=0)
    side = across(hidden_at[...], wide_proj, (1, 1))
    meta = rows_at[:, width:]
    wide = meta.astype(jnp.float32)
    lanes = lax.broadcasted_iota(jnp.int32, wide.shape, 1)
    is_route = (lanes >= rank + top) & (lanes < rank + 2 * top)
    named = (is_route & (wide == expert[0].astype(jnp.float32))).astype(jnp.float32)
    gate = jnp.sum(wide * pltpu.roll(named, LANES - top, 1), axis=1, keepdims=True)
    spread_from = lax.broadcasted_iota(jnp.int32, (LANES, rank * rank), 0)
    spread_to = lax.broadcasted_iota(jnp.int32, (LANES, rank * rank), 1) // rank
    spread = (spread_from == spread_to).astype(jnp.bfloat16)
    output_side = dot(meta, spread) * gate
    outer = output_side * jnp.concatenate([side] * (rank * rank // LANES), axis=1)
    doc = jnp.sum(jnp.where(lanes == rank + 2 * top, wide, 0.0), axis=1, keepdims=True)
    ids = lax.broadcasted_iota(jnp.int32, (wide.shape[0], docs_total), 1).astype(jnp.float32)
    table = (ids == doc).astype(jnp.bfloat16)
    high = outer.astype(jnp.bfloat16)
    low = (outer - high.astype(jnp.float32)).astype(jnp.bfloat16)
    total = total_in[...]
    for part in (high, low):
        total += across(table, part, (0, 0))
    if not folded:
        total_out[...] = total
        return
    for at in range(0, rank * rank, LANES):
        folded[0][:, at // LANES, :] = total[:, at : at + LANES]
    total_out[...] = folded[0][...].astype(total_out.dtype)


def sketch(pieces, expert, weights, proj, total, top, rank, fold=False):
    width, hidden = weights[0].shape
    rows, arrays, spots = 0, [], []
    for beside in pieces:
        for array, lead, column in beside:
            arrays.append(array)
            spots.append((lead, rows, column))
        rows += -(-beside[0][0].shape[1] // 16) * 16
    body = functools.partial(sketch_kernel, tuple(spots), top, rank, total.shape[0])
    vmem = pl.BlockSpec(memory_space=pltpu.VMEM)
    folded = (total.shape[0], rank * rank // LANES, LANES)
    result = jax.ShapeDtypeStruct(total.shape, jnp.float32)
    if fold:
        result = jax.ShapeDtypeStruct(folded, jnp.bfloat16)
    return pl.pallas_call(
        body,
        out_shape=result,
        in_specs=[pl.BlockSpec(memory_space=pltpu.SMEM)] + [vmem] * (len(arrays) + 4),
        out_specs=vmem,
        scratch_shapes=[
            pltpu.VMEM((rows, width + LANES), jnp.bfloat16),
            pltpu.VMEM((rows, hidden), jnp.bfloat16),
        ]
        + [pltpu.VMEM(folded, jnp.float32)] * fold,
        compiler_params=pltpu.CompilerParams(vmem_limit_bytes=14 * MIB),
        cost_estimate=LIGHT,
        name="sketch_rows",
    )(expert, *arrays, *weights, proj, total)


def on_device(tokens, out_grad, routes, gate_probs, doc_ids, w_gate, w_up, proj_hidden, proj_out):
    groups, planes = lax.axis_size("expert"), lax.axis_size("dp")
    devices = groups * planes
    row_count, width = tokens.shape
    top = routes.shape[1]
    rank = proj_out.shape[1]
    capacity = max(2, 3 * row_count * top // (2 * devices))
    me = lax.axis_index(AXES).astype(jnp.int32)

    def swap(value, hops):
        return lax.ppermute(value, AXES, [(i, i ^ hops[i & 1]) for i in range(devices)])

    def turn(value, by):
        pairs = [(((g + by) % groups, p), (g, p)) for g in range(groups) for p in range(planes)]
        return lax.ppermute(
            value, AXES, [(a * planes + b, c * planes + d) for (a, b), (c, d) in pairs]
        )

    ext = extend(tokens, out_grad, proj_out, routes, gate_probs, doc_ids)
    slots = [ext]
    for j in range(1, groups - 1):
        slots.append(turn(slots[-1], 1))
    slots.insert(groups - 2, turn(ext, groups - 1))
    bits = [1 << b for b in range(1, planes.bit_length() - 1)]
    shared = [[b for b in bits if b != bits[core]] for core in (0, 1)]
    side = jnp.where(me & 1 == 0, bits[0], bits[1]).astype(jnp.int32)
    targets = jnp.stack([me, me ^ 1, me ^ side, me ^ side ^ 1])
    *weights, held = hold(w_gate, w_up)
    total = jnp.zeros((devices, rank * rank), jnp.float32)
    own_id = me.reshape(1)
    args = (capacity, top, rank)

    def sketch_of(total, pieces, fold=False):
        return sketch(pieces, own_id, weights, proj_hidden.T, total, top, rank, fold)

    def gather(slot):
        sources = [slot]
        for hops in zip(*shared):
            sources += [swap(s, hops) for s in sources]
        return sources

    def spread(sources, after=own_id):
        own, other, further = compact(sources, targets, after, (1, 1, 2), *args)
        return [own, swap(other, (1, 1))], swap(further, bits)

    def spread_apart(sources):
        own, other, same, crossed = compact(sources, targets, own_id, (1, 1, 1, 1), *args)
        return [own, swap(other, (1, 1))], [swap(same, bits), swap(crossed, [b ^ 1 for b in bits])]

    def near(*pairs):
        return [[(array, 0, 0)] for pair in pairs for array in pair]

    def across_core(array):
        return [array, swap(array, (1, 1))]

    def far(*pairs):
        return [[piece] for a, b in pairs for piece in ((a, 0, 0), (b, 1, 0))]

    tied = lax.optimization_barrier
    near_now, far_now = spread(gather(slots[0]))
    near_kept, far_kept, far_now = [], [far_now], None
    for j in range(1, groups):
        sources, coming = gather(slots[j]), slots[j + 1 : j + 2]
        if j == groups - 1:
            total = sketch_of(total, near(near_kept, near_now) + far(*map(across_core, far_old)))
            near_kept, near_now = [], []
        group = (near_now, far_kept, sources, coming, [total] if j != 2 else [held])
        near_now, far_kept, sources, slots[j + 1 : j + 2], kept = tied(group)
        near_kept += near_now
        if j == groups - 1:
            near_now, far_next = spread_apart(sources)
            total = kept[0]
        else:
            near_now, far_next = spread(sources, kept[0] if j == 2 else own_id)
        if j == 1:
            far_old = far_kept
            far_kept = []
        elif far_now is not None:
            far_kept = far_kept + [far_now]
        far_now = far_next
    near_now, far_kept = tied((near_now, far_kept))
    total = sketch_of(total, near(near_kept, near_now) + far(*map(across_core, far_kept)))
    far_now, total = tied((far_now, total))
    folded = sketch_of(total, near(far_now), True)
    owned = lax.all_to_all(folded, AXES, split_axis=0, concat_axis=0, tiled=True)
    return owned.reshape(1, devices, rank * rank).astype(jnp.float32)


def solution(mesh):
    placed = (
        P(AXES, None),
        P(AXES, None),
        P(AXES, None),
        P(AXES, None),
        P(AXES),
        P(AXES, None, None),
        P(AXES, None, None),
        P(),
        P(),
    )
    return jax.shard_map(
        on_device,
        mesh=mesh,
        in_specs=placed,
        out_specs=P(AXES, None, None),
        check_vma=False,
    )
```

```python
import functools

import jax
import jax.numpy as jnp
from jax import lax
from jax.experimental import pallas as pl
from jax.experimental.pallas import tpu as pltpu
from jax.sharding import PartitionSpec as P

AXES = ("expert", "dp")
LANES = 128
MIB = 1 << 20
LIGHT = pl.CostEstimate(flops=1, bytes_accessed=1, transcendentals=0)


def place(width, first):
    rows = lax.broadcasted_iota(jnp.int32, (width, LANES), 0)
    lanes = lax.broadcasted_iota(jnp.int32, (width, LANES), 1)
    return (lanes == rows + first).astype(jnp.bfloat16)


def dot(a, b):
    return jnp.dot(a, b, preferred_element_type=jnp.float32)


def across(a, b, over):
    return lax.dot_general(a, b, ((over[:1], over[1:]), ((), ())), preferred_element_type=jnp.float32)


def extend_kernel(rank, top, tokens, *refs):
    sources, out, held, sems = refs[:5], refs[5], refs[6:11], refs[11]
    width = tokens.shape[1]
    copies = [pltpu.make_async_copy(a, b, sems.at[i]) for i, (a, b) in enumerate(zip(sources, held))]
    copies.append(pltpu.make_async_copy(tokens, out.at[:, :width], sems.at[5]))
    for copy in copies:
        copy.start()
    for copy in copies[:-1]:
        copy.wait()
    grads, proj, routes, gates, docs = held
    small = jnp.float32
    projected = across(grads[...], proj[...], (1, 1)).astype(jnp.bfloat16)
    meta = dot(projected, place(rank, 0))
    meta += across(gates[...], place(top, rank), (0, 0))
    meta += across(routes[...].astype(small).astype(jnp.bfloat16), place(top, rank + top), (0, 0))
    doc = jnp.concatenate([docs[...].astype(small)] * 8, axis=0).astype(jnp.bfloat16)
    meta += across(doc, place(8, rank + 2 * top), (0, 0))
    out[:, width:] = meta.astype(jnp.bfloat16)
    copies[-1].wait()


def extend(tokens, out_grad, proj_out, routes, gate_probs, doc_ids):
    rows, width = tokens.shape
    body = functools.partial(extend_kernel, proj_out.shape[1], routes.shape[1])
    operands = [tokens, out_grad, proj_out.T, routes.T, gate_probs.T, doc_ids.reshape(1, rows)]
    return pl.pallas_call(
        body,
        out_shape=jax.ShapeDtypeStruct((rows, width + LANES), jnp.bfloat16),
        in_specs=[pl.BlockSpec(memory_space=pltpu.HBM)] * len(operands),
        out_specs=pl.BlockSpec(memory_space=pltpu.VMEM),
        scratch_shapes=[pltpu.VMEM(o.shape, o.dtype) for o in operands[1:]]
        + [pltpu.SemaphoreType.DMA((len(operands),))],
        compiler_params=pltpu.CompilerParams(vmem_limit_bytes=4 * MIB),
        name="extend_rows",
    )(*[pltpu.with_memory_space_constraint(o, pltpu.HBM) for o in operands])


def position(planes):
    return (lax.axis_index("expert") * planes + lax.axis_index("dp")).astype(jnp.int32)


def compact_kernel(spots, sides, planes, capacity, top, rank, after, *refs):
    me = position(planes)
    side = jnp.where(me & 1 == 0, sides[0], sides[1])
    targets = [me, me ^ 1, me ^ side, me ^ side ^ 1]
    parts = 1 + spots[-1][0]
    sources, outs = refs[:-parts], refs[-parts:]
    count = len(sources)
    rows, total = sources[0].shape
    width = total - LANES
    meta = jnp.concatenate([s[:, width:] for s in sources], axis=0).astype(jnp.float32)
    lanes = lax.broadcasted_iota(jnp.int32, meta.shape, 1)
    is_route = (lanes >= rank + top) & (lanes < rank + 2 * top)
    hits = jnp.zeros(meta.shape, jnp.float32)
    for q in range(4):
        named = is_route & (meta == targets[q].astype(jnp.float32))
        hit = jnp.sum(named.astype(jnp.float32), axis=1, keepdims=True)
        hits = jnp.where(lanes == q, hit, hits)
    every = count * rows
    here = lax.broadcasted_iota(jnp.int32, (every, every), 0)
    other = lax.broadcasted_iota(jnp.int32, (every, every), 1)
    earlier = ((other < here) & (other // rows == here // rows)).astype(jnp.bfloat16)
    before = dot(earlier, hits.astype(jnp.bfloat16))
    first = lax.broadcasted_iota(jnp.int32, meta.shape, 0) // rows * capacity
    slots = jnp.where(hits > 0, before + first.astype(jnp.float32), -1.0).T
    picked = count * capacity
    spot = lax.broadcasted_iota(jnp.int32, (picked, every), 0).astype(jnp.float32)
    pick = jnp.concatenate(
        [(spot == slots[q : q + 1, :]).astype(jnp.bfloat16) for q in range(4)], axis=0
    )
    step = 4 * LANES
    for at in range(0, total, step):
        end = min(at + step, total)
        found = dot(pick, jnp.concatenate([s[:, at:end] for s in sources], axis=0))
        for q, (out, lead) in enumerate(spots):
            part = found[q * picked : (q + 1) * picked].astype(jnp.bfloat16)
            outs[out][lead, :, at:end] = part


def compact(sources, after, leads, sides, planes, capacity, top, rank):
    spots = tuple((i, lead) for i, n in enumerate(leads) for lead in range(n))
    body = functools.partial(compact_kernel, spots, sides, planes, capacity, top, rank)
    rows, width = len(sources) * capacity, sources[0].shape[1]
    return pl.pallas_call(
        body,
        out_shape=[jax.ShapeDtypeStruct((n, rows, width), jnp.bfloat16) for n in leads],
        in_specs=[pl.BlockSpec(memory_space=pl.ANY)]
        + [pl.BlockSpec(memory_space=pltpu.VMEM)] * len(sources),
        out_specs=[pl.BlockSpec(memory_space=pltpu.VMEM)] * len(leads),
        compiler_params=pltpu.CompilerParams(vmem_limit_bytes=8 * MIB),
        cost_estimate=LIGHT,
        name="compact_rows",
    )(after, *sources)


def hold_kernel(gate_w, up_w, gate_out, up_out, done, sems):
    copies = [
        pltpu.make_async_copy(gate_w.at[0], gate_out, sems.at[0]),
        pltpu.make_async_copy(up_w.at[0], up_out, sems.at[1]),
    ]
    for copy in copies:
        copy.start()
    for copy in copies:
        copy.wait()
    done[0] = 0


def hold(w_gate, w_up):
    shape = w_gate.shape[1:]
    return pl.pallas_call(
        hold_kernel,
        out_shape=[pltpu.VMEM(shape, jnp.bfloat16)] * 2 + [jax.ShapeDtypeStruct((1,), jnp.int32)],
        in_specs=[pl.BlockSpec(memory_space=pltpu.HBM)] * 2,
        out_specs=[pl.BlockSpec(memory_space=pltpu.VMEM)] * 2
        + [pl.BlockSpec(memory_space=pltpu.SMEM)],
        scratch_shapes=[pltpu.SemaphoreType.DMA((2,))],
        compiler_params=pltpu.CompilerParams(vmem_limit_bytes=2 * MIB),
        cost_estimate=LIGHT,
        name="hold_weights",
    )(*[pltpu.with_memory_space_constraint(w, pltpu.HBM) for w in (w_gate, w_up)])


def sketch_kernel(spots, planes, top, rank, docs_total, *refs):
    pieces = refs[: len(spots)]
    gate_w, up_w, proj, total_in, total_out, rows_at, hidden_at, *folded = refs[len(spots) :]
    width, hidden = gate_w.shape
    for ref, (lead, row, column) in zip(pieces, spots):
        r, c = ref.shape[1:]
        if r % 16:
            below = row + r // 16 * 16
            rows_at[below : below + 16, column : column + c] = jnp.zeros((16, c), jnp.bfloat16)
        rows_at[row : row + r, column : column + c] = ref[lead]

    rows = rows_at[:, :width]
    tile = 256
    for at in range(0, hidden, tile):
        gate_part = dot(rows, gate_w[:, at : at + tile])
        up_part = dot(rows, up_w[:, at : at + tile])
        value = gate_part / (1.0 + jnp.exp(-gate_part)) * up_part
        hidden_at[:, at : at + tile] = value.astype(jnp.bfloat16)

    wide_proj = jnp.concatenate([proj[...]] * (LANES // rank), axis=0)
    side = across(hidden_at[...], wide_proj, (1, 1))
    meta = rows_at[:, width:]
    wide = meta.astype(jnp.float32)
    lanes = lax.broadcasted_iota(jnp.int32, wide.shape, 1)
    is_route = (lanes >= rank + top) & (lanes < rank + 2 * top)
    named = (is_route & (wide == position(planes).astype(jnp.float32))).astype(jnp.float32)
    gate = jnp.sum(wide * pltpu.roll(named, LANES - top, 1), axis=1, keepdims=True)
    spread_from = lax.broadcasted_iota(jnp.int32, (LANES, rank * rank), 0)
    spread_to = lax.broadcasted_iota(jnp.int32, (LANES, rank * rank), 1) // rank
    spread = (spread_from == spread_to).astype(jnp.bfloat16)
    output_side = dot(meta, spread) * gate
    outer = output_side * jnp.concatenate([side] * (rank * rank // LANES), axis=1)
    doc = jnp.sum(jnp.where(lanes == rank + 2 * top, wide, 0.0), axis=1, keepdims=True)
    ids = lax.broadcasted_iota(jnp.int32, (wide.shape[0], docs_total), 1).astype(jnp.float32)
    table = (ids == doc).astype(jnp.bfloat16)
    high = outer.astype(jnp.bfloat16)
    low = (outer - high.astype(jnp.float32)).astype(jnp.bfloat16)
    total = total_in[...]
    for part in (high, low):
        total += across(table, part, (0, 0))
    if not folded:
        total_out[...] = total
        return
    for at in range(0, rank * rank, LANES):
        folded[0][:, at // LANES, :] = total[:, at : at + LANES]
    total_out[...] = folded[0][...].astype(total_out.dtype)


def sketch(pieces, weights, proj, total, planes, top, rank, fold=False):
    width, hidden = weights[0].shape
    rows, arrays, spots = 0, [], []
    for beside in pieces:
        for array, lead, column in beside:
            arrays.append(array)
            spots.append((lead, rows, column))
        rows += -(-beside[0][0].shape[1] // 16) * 16
    body = functools.partial(sketch_kernel, tuple(spots), planes, top, rank, total.shape[0])
    vmem = pl.BlockSpec(memory_space=pltpu.VMEM)
    folded = (total.shape[0], rank * rank // LANES, LANES)
    result = jax.ShapeDtypeStruct(total.shape, jnp.float32)
    if fold:
        result = jax.ShapeDtypeStruct(folded, jnp.bfloat16)
    return pl.pallas_call(
        body,
        out_shape=result,
        in_specs=[vmem] * (len(arrays) + 4),
        out_specs=vmem,
        scratch_shapes=[
            pltpu.VMEM((rows, width + LANES), jnp.bfloat16),
            pltpu.VMEM((rows, hidden), jnp.bfloat16),
        ]
        + [pltpu.VMEM(folded, jnp.float32)] * fold,
        compiler_params=pltpu.CompilerParams(vmem_limit_bytes=14 * MIB),
        cost_estimate=LIGHT,
        name="sketch_rows",
    )(*arrays, *weights, proj, total)


def on_device(tokens, out_grad, routes, gate_probs, doc_ids, w_gate, w_up, proj_hidden, proj_out):
    groups, planes = lax.axis_size("expert"), lax.axis_size("dp")
    devices = groups * planes
    row_count, width = tokens.shape
    top = routes.shape[1]
    rank = proj_out.shape[1]
    capacity = max(2, 3 * row_count * top // (2 * devices))

    def swap(value, hops):
        return lax.ppermute(value, AXES, [(i, i ^ hops[i & 1]) for i in range(devices)])

    def turn(value, by):
        pairs = [(((g + by) % groups, p), (g, p)) for g in range(groups) for p in range(planes)]
        return lax.ppermute(
            value, AXES, [(a * planes + b, c * planes + d) for (a, b), (c, d) in pairs]
        )

    ext = extend(tokens, out_grad, proj_out, routes, gate_probs, doc_ids)
    slots = [ext]
    for j in range(1, groups - 1):
        slots.append(turn(slots[-1], 1))
    slots.insert(groups - 2, turn(ext, groups - 1))
    bits = [1 << b for b in range(1, planes.bit_length() - 1)]
    shared = [[b for b in bits if b != bits[core]] for core in (0, 1)]
    *weights, held = hold(w_gate, w_up)
    total = jnp.zeros((devices, rank * rank), jnp.float32)
    own_id = jnp.zeros((1,), jnp.int32)
    args = (tuple(bits[:2]), planes, capacity, top, rank)

    def sketch_of(total, pieces, fold=False):
        return sketch(pieces, weights, proj_hidden.T, total, planes, top, rank, fold)

    def gather(slot):
        sources = [slot]
        for hops in zip(*shared):
            sources += [swap(s, hops) for s in sources]
        return sources

    def spread(sources, after=own_id):
        own, other, further = compact(sources, after, (1, 1, 2), *args)
        return [own, swap(other, (1, 1))], swap(further, bits)

    def spread_apart(sources):
        own, other, same, crossed = compact(sources, own_id, (1, 1, 1, 1), *args)
        return [own, swap(other, (1, 1))], [swap(same, bits), swap(crossed, [b ^ 1 for b in bits])]

    def near(*pairs):
        return [[(array, 0, 0)] for pair in pairs for array in pair]

    def across_core(array):
        return [array, swap(array, (1, 1))]

    def far(*pairs):
        return [[piece] for a, b in pairs for piece in ((a, 0, 0), (b, 1, 0))]

    tied = lax.optimization_barrier
    near_now, far_now = spread(gather(slots[0]))
    near_kept, far_kept, far_now = [], [far_now], None
    for j in range(1, groups):
        sources, coming = gather(slots[j]), slots[j + 1 : j + 2]
        if j == groups - 1:
            total = sketch_of(total, near(near_kept, near_now) + far(*map(across_core, far_old)))
            near_kept, near_now = [], []
        group = (near_now, far_kept, sources, coming, [total] if j != 2 else [held])
        near_now, far_kept, sources, slots[j + 1 : j + 2], kept = tied(group)
        near_kept += near_now
        if j == groups - 1:
            near_now, far_next = spread_apart(sources)
            total = kept[0]
        else:
            near_now, far_next = spread(sources, kept[0] if j == 2 else own_id)
        if j == 1:
            far_old = far_kept
            far_kept = []
        elif far_now is not None:
            far_kept = far_kept + [far_now]
        far_now = far_next
    near_now, far_kept = tied((near_now, far_kept))
    total = sketch_of(total, near(near_kept, near_now) + far(*map(across_core, far_kept)))
    far_now, total = tied((far_now, total))
    folded = sketch_of(total, near(far_now), True)
    owned = lax.all_to_all(folded, AXES, split_axis=0, concat_axis=0, tiled=True)
    return owned.reshape(1, devices, rank * rank).astype(jnp.float32)


def solution(mesh):
    placed = (
        P(AXES, None),
        P(AXES, None),
        P(AXES, None),
        P(AXES, None),
        P(AXES),
        P(AXES, None, None),
        P(AXES, None, None),
        P(),
        P(),
    )
    return jax.shard_map(
        on_device,
        mesh=mesh,
        in_specs=placed,
        out_specs=P(AXES, None, None),
        check_vma=False,
    )
```

```python
import functools

import jax
import jax.numpy as jnp
from jax import lax
from jax.experimental import pallas as pl
from jax.experimental.pallas import tpu as pltpu
from jax.sharding import PartitionSpec as P

AXES = ("expert", "dp")
LANES = 128
MIB = 1 << 20
LIGHT = pl.CostEstimate(flops=1, bytes_accessed=1, transcendentals=0)


def place(width, first):
    rows = lax.broadcasted_iota(jnp.int32, (width, LANES), 0)
    lanes = lax.broadcasted_iota(jnp.int32, (width, LANES), 1)
    return (lanes == rows + first).astype(jnp.bfloat16)


def dot(a, b):
    return jnp.dot(a, b, preferred_element_type=jnp.float32)


def across(a, b, over):
    return lax.dot_general(a, b, ((over[:1], over[1:]), ((), ())), preferred_element_type=jnp.float32)


def extend_kernel(rank, top, tokens, *refs):
    sources, out, held, sems = refs[:5], refs[5], refs[6:11], refs[11]
    width = tokens.shape[1]
    copies = [pltpu.make_async_copy(a, b, sems.at[i]) for i, (a, b) in enumerate(zip(sources, held))]
    copies.append(pltpu.make_async_copy(tokens, out.at[:, :width], sems.at[5]))
    for copy in copies:
        copy.start()
    for copy in copies[:-1]:
        copy.wait()
    grads, proj, routes, gates, docs = held
    small = jnp.float32
    projected = across(grads[...], proj[...], (1, 1)).astype(jnp.bfloat16)
    meta = dot(projected, place(rank, 0))
    meta += across(gates[...], place(top, rank), (0, 0))
    meta += across(routes[...].astype(small).astype(jnp.bfloat16), place(top, rank + top), (0, 0))
    doc = jnp.concatenate([docs[...].astype(small)] * 8, axis=0).astype(jnp.bfloat16)
    meta += across(doc, place(8, rank + 2 * top), (0, 0))
    out[:, width:] = meta.astype(jnp.bfloat16)
    copies[-1].wait()


def extend(tokens, out_grad, proj_out, routes, gate_probs, doc_ids):
    rows, width = tokens.shape
    body = functools.partial(extend_kernel, proj_out.shape[1], routes.shape[1])
    operands = [tokens, out_grad, proj_out.T, routes.T, gate_probs.T, doc_ids.reshape(1, rows)]
    return pl.pallas_call(
        body,
        out_shape=jax.ShapeDtypeStruct((rows, width + LANES), jnp.bfloat16),
        in_specs=[pl.BlockSpec(memory_space=pltpu.HBM)] * len(operands),
        out_specs=pl.BlockSpec(memory_space=pltpu.VMEM),
        scratch_shapes=[pltpu.VMEM(o.shape, o.dtype) for o in operands[1:]]
        + [pltpu.SemaphoreType.DMA((len(operands),))],
        compiler_params=pltpu.CompilerParams(vmem_limit_bytes=4 * MIB),
        name="extend_rows",
    )(*[pltpu.with_memory_space_constraint(o, pltpu.HBM) for o in operands])


def position(planes):
    return (lax.axis_index("expert") * planes + lax.axis_index("dp")).astype(jnp.int32)


def compact_kernel(spots, sides, planes, capacity, top, rank, after, *refs):
    me = position(planes)
    side = jnp.where(me & 1 == 0, sides[0], sides[1])
    targets = [me, me ^ 1, me ^ side, me ^ side ^ 1]
    parts = 1 + spots[-1][0]
    sources, outs = refs[:-parts], refs[-parts:]
    count = len(sources)
    rows, total = sources[0].shape
    width = total - LANES
    meta = jnp.concatenate([s[:, width:] for s in sources], axis=0).astype(jnp.float32)
    lanes = lax.broadcasted_iota(jnp.int32, meta.shape, 1)
    is_route = (lanes >= rank + top) & (lanes < rank + 2 * top)
    named = [is_route & (meta == targets[q].astype(jnp.float32)) for q in range(4)]
    named = jnp.concatenate([n.astype(jnp.float32).astype(jnp.bfloat16) for n in named], axis=1)
    expert = lax.broadcasted_iota(jnp.int32, (8, 4 * LANES), 0)
    column = lax.broadcasted_iota(jnp.int32, (8, 4 * LANES), 1)
    hits = across((expert == column // LANES).astype(jnp.bfloat16), named, (1, 1))
    every = count * rows
    other = lax.broadcasted_iota(jnp.int32, (every, every), 0)
    here = lax.broadcasted_iota(jnp.int32, (every, every), 1)
    earlier = ((other < here) & (other // rows == here // rows)).astype(jnp.bfloat16)
    before = dot(hits.astype(jnp.bfloat16), earlier)
    first = lax.broadcasted_iota(jnp.int32, hits.shape, 1) // rows * capacity
    slots = jnp.where(hits > 0, before + first.astype(jnp.float32), -1.0)
    picked = count * capacity
    spot = lax.broadcasted_iota(jnp.int32, (picked, every), 0).astype(jnp.float32)
    pick = jnp.concatenate(
        [(spot == slots[q : q + 1, :]).astype(jnp.bfloat16) for q in range(4)], axis=0
    )
    step = 4 * LANES
    for at in range(0, total, step):
        end = min(at + step, total)
        found = dot(pick, jnp.concatenate([s[:, at:end] for s in sources], axis=0))
        for q, (out, lead) in enumerate(spots):
            part = found[q * picked : (q + 1) * picked].astype(jnp.bfloat16)
            outs[out][lead, :, at:end] = part


def compact(sources, after, leads, sides, planes, capacity, top, rank):
    spots = tuple((i, lead) for i, n in enumerate(leads) for lead in range(n))
    body = functools.partial(compact_kernel, spots, sides, planes, capacity, top, rank)
    rows, width = len(sources) * capacity, sources[0].shape[1]
    return pl.pallas_call(
        body,
        out_shape=[jax.ShapeDtypeStruct((n, rows, width), jnp.bfloat16) for n in leads],
        in_specs=[pl.BlockSpec(memory_space=pl.ANY)]
        + [pl.BlockSpec(memory_space=pltpu.VMEM)] * len(sources),
        out_specs=[pl.BlockSpec(memory_space=pltpu.VMEM)] * len(leads),
        compiler_params=pltpu.CompilerParams(vmem_limit_bytes=8 * MIB),
        cost_estimate=LIGHT,
        name="compact_rows",
    )(after, *sources)


def hold_kernel(gate_w, up_w, gate_out, up_out, done, sems):
    copies = [
        pltpu.make_async_copy(gate_w.at[0], gate_out, sems.at[0]),
        pltpu.make_async_copy(up_w.at[0], up_out, sems.at[1]),
    ]
    for copy in copies:
        copy.start()
    for copy in copies:
        copy.wait()
    done[0] = 0


def hold(w_gate, w_up):
    shape = w_gate.shape[1:]
    return pl.pallas_call(
        hold_kernel,
        out_shape=[pltpu.VMEM(shape, jnp.bfloat16)] * 2 + [jax.ShapeDtypeStruct((1,), jnp.int32)],
        in_specs=[pl.BlockSpec(memory_space=pltpu.HBM)] * 2,
        out_specs=[pl.BlockSpec(memory_space=pltpu.VMEM)] * 2
        + [pl.BlockSpec(memory_space=pltpu.SMEM)],
        scratch_shapes=[pltpu.SemaphoreType.DMA((2,))],
        compiler_params=pltpu.CompilerParams(vmem_limit_bytes=2 * MIB),
        cost_estimate=LIGHT,
        name="hold_weights",
    )(*[pltpu.with_memory_space_constraint(w, pltpu.HBM) for w in (w_gate, w_up)])


def sketch_kernel(spots, planes, top, rank, docs_total, *refs):
    pieces = refs[: len(spots)]
    gate_w, up_w, proj, total_in, total_out, rows_at, hidden_at, *folded = refs[len(spots) :]
    width, hidden = gate_w.shape
    for ref, (lead, row, column) in zip(pieces, spots):
        r, c = ref.shape[1:]
        if r % 16:
            below = row + r // 16 * 16
            rows_at[below : below + 16, column : column + c] = jnp.zeros((16, c), jnp.bfloat16)
        rows_at[row : row + r, column : column + c] = ref[lead]

    rows = rows_at[:, :width]
    tile = 256
    for at in range(0, hidden, tile):
        gate_part = dot(rows, gate_w[:, at : at + tile])
        up_part = dot(rows, up_w[:, at : at + tile])
        value = gate_part / (1.0 + jnp.exp(-gate_part)) * up_part
        hidden_at[:, at : at + tile] = value.astype(jnp.bfloat16)

    wide_proj = jnp.concatenate([proj[...]] * (LANES // rank), axis=0)
    side = across(hidden_at[...], wide_proj, (1, 1))
    meta = rows_at[:, width:]
    wide = meta.astype(jnp.float32)
    lanes = lax.broadcasted_iota(jnp.int32, wide.shape, 1)
    is_route = (lanes >= rank + top) & (lanes < rank + 2 * top)
    named = (is_route & (wide == position(planes).astype(jnp.float32))).astype(jnp.float32)
    gate = jnp.sum(wide * pltpu.roll(named, LANES - top, 1), axis=1, keepdims=True)
    spread_from = lax.broadcasted_iota(jnp.int32, (LANES, rank * rank), 0)
    spread_to = lax.broadcasted_iota(jnp.int32, (LANES, rank * rank), 1) // rank
    spread = (spread_from == spread_to).astype(jnp.bfloat16)
    output_side = dot(meta, spread) * gate
    outer = output_side * jnp.concatenate([side] * (rank * rank // LANES), axis=1)
    doc = jnp.sum(jnp.where(lanes == rank + 2 * top, wide, 0.0), axis=1, keepdims=True)
    ids = lax.broadcasted_iota(jnp.int32, (wide.shape[0], docs_total), 1).astype(jnp.float32)
    table = (ids == doc).astype(jnp.bfloat16)
    high = outer.astype(jnp.bfloat16)
    low = (outer - high.astype(jnp.float32)).astype(jnp.bfloat16)
    total = total_in[...]
    for part in (high, low):
        total += across(table, part, (0, 0))
    if not folded:
        total_out[...] = total
        return
    for at in range(0, rank * rank, LANES):
        folded[0][:, at // LANES, :] = total[:, at : at + LANES]
    total_out[...] = folded[0][...].astype(total_out.dtype)


def sketch(pieces, weights, proj, total, planes, top, rank, fold=False):
    width, hidden = weights[0].shape
    rows, arrays, spots = 0, [], []
    for beside in pieces:
        for array, lead, column in beside:
            arrays.append(array)
            spots.append((lead, rows, column))
        rows += -(-beside[0][0].shape[1] // 16) * 16
    body = functools.partial(sketch_kernel, tuple(spots), planes, top, rank, total.shape[0])
    vmem = pl.BlockSpec(memory_space=pltpu.VMEM)
    folded = (total.shape[0], rank * rank // LANES, LANES)
    result = jax.ShapeDtypeStruct(total.shape, jnp.float32)
    if fold:
        result = jax.ShapeDtypeStruct(folded, jnp.bfloat16)
    return pl.pallas_call(
        body,
        out_shape=result,
        in_specs=[vmem] * (len(arrays) + 4),
        out_specs=vmem,
        scratch_shapes=[
            pltpu.VMEM((rows, width + LANES), jnp.bfloat16),
            pltpu.VMEM((rows, hidden), jnp.bfloat16),
        ]
        + [pltpu.VMEM(folded, jnp.float32)] * fold,
        compiler_params=pltpu.CompilerParams(vmem_limit_bytes=14 * MIB),
        cost_estimate=LIGHT,
        name="sketch_rows",
    )(*arrays, *weights, proj, total)


def on_device(tokens, out_grad, routes, gate_probs, doc_ids, w_gate, w_up, proj_hidden, proj_out):
    groups, planes = lax.axis_size("expert"), lax.axis_size("dp")
    devices = groups * planes
    row_count, width = tokens.shape
    top = routes.shape[1]
    rank = proj_out.shape[1]
    capacity = max(2, 3 * row_count * top // (2 * devices))

    def swap(value, hops):
        return lax.ppermute(value, AXES, [(i, i ^ hops[i & 1]) for i in range(devices)])

    def turn(value, by):
        pairs = [(((g + by) % groups, p), (g, p)) for g in range(groups) for p in range(planes)]
        return lax.ppermute(
            value, AXES, [(a * planes + b, c * planes + d) for (a, b), (c, d) in pairs]
        )

    ext = extend(tokens, out_grad, proj_out, routes, gate_probs, doc_ids)
    slots = [ext]
    for j in range(1, groups - 1):
        slots.append(turn(slots[-1], 1))
    slots.insert(groups - 2, turn(ext, groups - 1))
    bits = [1 << b for b in range(1, planes.bit_length() - 1)]
    shared = [[b for b in bits if b != bits[core]] for core in (0, 1)]
    *weights, held = hold(w_gate, w_up)
    total = jnp.zeros((devices, rank * rank), jnp.float32)
    own_id = jnp.zeros((1,), jnp.int32)
    args = (tuple(bits[:2]), planes, capacity, top, rank)

    def sketch_of(total, pieces, fold=False):
        return sketch(pieces, weights, proj_hidden.T, total, planes, top, rank, fold)

    def gather(slot):
        sources = [slot]
        for hops in zip(*shared):
            sources += [swap(s, hops) for s in sources]
        return sources

    def spread(sources, after=own_id):
        own, other, further = compact(sources, after, (1, 1, 2), *args)
        return [own, swap(other, (1, 1))], swap(further, bits)

    def spread_apart(sources):
        own, other, same, crossed = compact(sources, own_id, (1, 1, 1, 1), *args)
        return [own, swap(other, (1, 1))], [swap(same, bits), swap(crossed, [b ^ 1 for b in bits])]

    def near(*pairs):
        return [[(array, 0, 0)] for pair in pairs for array in pair]

    def across_core(array):
        return [array, swap(array, (1, 1))]

    def far(*pairs):
        return [[piece] for a, b in pairs for piece in ((a, 0, 0), (b, 1, 0))]

    tied = lax.optimization_barrier
    near_now, far_now = spread(gather(slots[0]))
    near_kept, far_kept, far_now = [], [far_now], None
    for j in range(1, groups):
        sources, coming = gather(slots[j]), slots[j + 1 : j + 2]
        if j == groups - 1:
            total = sketch_of(total, near(near_kept, near_now) + far(*map(across_core, far_old)))
            near_kept, near_now = [], []
        group = (near_now, far_kept, sources, coming, [total] if j != 2 else [held])
        near_now, far_kept, sources, slots[j + 1 : j + 2], kept = tied(group)
        near_kept += near_now
        if j == groups - 1:
            near_now, far_next = spread_apart(sources)
            total = kept[0]
        else:
            near_now, far_next = spread(sources, kept[0] if j == 2 else own_id)
        if j == 1:
            far_old = far_kept
            far_kept = []
        elif far_now is not None:
            far_kept = far_kept + [far_now]
        far_now = far_next
    near_now, far_kept = tied((near_now, far_kept))
    total = sketch_of(total, near(near_kept, near_now) + far(*map(across_core, far_kept)))
    far_now, total = tied((far_now, total))
    folded = sketch_of(total, near(far_now), True)
    owned = lax.all_to_all(folded, AXES, split_axis=0, concat_axis=0, tiled=True)
    return owned.reshape(1, devices, rank * rank).astype(jnp.float32)


def solution(mesh):
    placed = (
        P(AXES, None),
        P(AXES, None),
        P(AXES, None),
        P(AXES, None),
        P(AXES),
        P(AXES, None, None),
        P(AXES, None, None),
        P(),
        P(),
    )
    return jax.shard_map(
        on_device,
        mesh=mesh,
        in_specs=placed,
        out_specs=P(AXES, None, None),
        check_vma=False,
    )
```
